32 devices in a mesh: ctx: 8 (over z, y), tp: 4 (over x, core).
Axes of the slice: x: 2, y: 2, z: 4, core: 2. Of those that a mesh axis runs over, the one named last changes fastest.
Arguments:
- hidden_in: bfloat16 [2, 6656, 1024], P(None, ('ctx', 'tp')), may hold values from -6 to 6
- norm1_gain: float32 [1024], replicated, may hold values from 0.1 to 1.9
- qkv_weight: bfloat16 [1024, 3, 16, 64], P(None, None, 'tp'), may hold values from -0.1875 to 0.1875
- attn_weight: bfloat16 [16, 64, 1024], P('tp'), may hold values from -1 to 1
- norm2_gain: float32 [1024], replicated, may hold values from 0.1 to 1.9
- ffn_in_weight: bfloat16 [1024, 2, 2624], P(None, None, 'tp'), may hold values from -0.1875 to 0.1875
- ffn_out_weight: bfloat16 [2624, 1024], P('tp'), may hold values from -0.125 to 0.125
- doc_ids: int32 [2, 6656], P(None, 'ctx'), may hold values from 0 to 4, as said below
- out_grad: bfloat16 [2, 6656, 1024], P(None, ('ctx', 'tp')), may hold values from -6 to 6
Outputs:
- block_out: bfloat16 [2, 6656, 1024], P(None, ('ctx', 'tp'))
- in_grad: bfloat16 [2, 6656, 1024], P(None, ('ctx', 'tp'))
- norm1_gain_grad: float32 [1024], replicated
- qkv_weight_grad: float32 [1024, 3, 16, 64], P(None, None, 'tp')
- attn_weight_grad: float32 [16, 64, 1024], P('tp')
- norm2_gain_grad: float32 [1024], replicated
- ffn_in_weight_grad: float32 [1024, 2, 2624], P(None, None, 'tp')
- ffn_out_weight_grad: float32 [2624, 1024], P('tp')
The draws below stay inside these ranges and needn't reach their ends.
Inputs may be any that keep to these rules, and one draw needn't show every extreme that they name: `doc_ids`: within each sequence the document numbers start at 0 and rise by one at each document start; one sequence, which one varying with the seed, is a single document over all 6656 tokens, and every other sequence holds exactly 5 documents.
All inputs are finite; a program needn't handle non-finite values.
Results may differ from the reference program's by a relative error of at most 0.024.
Values may be sent and summed in bfloat16 or wider, within the bound.
No kernel may reach another device: no remote copies, remote signals or barrier semaphores. Data moves between devices by JAX's collectives and lax.ppermute only.
A program may use at most 640 MiB of HBM per device.

```python
import math
import jax
import jax.numpy as jnp
from jax import lax

D = 1024
HEADS = 16
HD = 64
FF = 2624
NSEQ = 2
LEN = 6656


def draw_doc_ids(key, part):
    key = jax.random.fold_in(key, 7)
    first, second = jax.random.split(key)
    row_keys = jax.random.split(first, NSEQ)
    places = jnp.arange(LEN, dtype=jnp.int32)

    def one_row(row_key):
        picks = jax.random.permutation(row_key, LEN - 1)[:4].astype(jnp.int32) + 1
        return jnp.sum((places[:, None] == picks[None, :]).astype(jnp.int32), axis=1)
    cuts = jax.vmap(one_row)(row_keys)
    whole = jax.random.randint(second, (), 0, NSEQ)
    keep = (jnp.arange(NSEQ) != whole).astype(jnp.int32)[:, None]
    return jnp.cumsum(cuts * keep, axis=1).astype(jnp.int32)


def block_levels(key, extent, cuts, low, largest):
    level = 1.0
    for dim, blocks in cuts:
        heights = jax.random.uniform(jax.random.fold_in(jax.random.fold_in(key, 6), dim), (blocks,), jnp.float32, low / len(cuts), largest / len(cuts))
        level = level * jnp.repeat(jnp.exp(heights), extent[dim] // blocks).reshape((-1,) + (1,) * (len(extent) - 1 - dim))
    return level


def centred(key, extent, spread, most, shards=(), held_as=jnp.bfloat16):
    factor_of = block_levels(key, extent, shards, -0.22, 0.18) if shards else 1.0
    array = jax.random.normal(key, extent, jnp.float32) * spread * factor_of
    return jnp.minimum(jnp.maximum(array, -most), most).astype(held_as)


def setup_inputs(seed: int = 0) -> dict:
    splits = jax.random.split(jax.random.key(seed), 10)
    hidden_in = centred(splits[0], (NSEQ, LEN, D), 1.0, 6.0, ((1, 32),))
    norm1_gain = jnp.clip(1.0 + 0.18 * jax.random.normal(splits[1], (D,), jnp.float32), 0.1, 1.9)
    qkv_weight = centred(splits[2], (D, 3, HEADS, HD), D ** -0.5, 0.1875, ((2, 4),))
    attn_weight = centred(splits[3], (HEADS, HD, D), (max(HEADS * HD * 256 // LEN, 1)) ** -0.5, 1.0, ((0, 4),))
    norm2_gain = jnp.clip(1.0 + 0.18 * jax.random.normal(splits[4], (D,), jnp.float32), 0.1, 1.9)
    ffn_in_weight = centred(splits[5], (D, 2, FF), D ** -0.5, 0.1875, ((2, 4),))
    ffn_out_weight = centred(splits[6], (FF, D), FF ** -0.5, 0.125, ((0, 4),))
    doc_ids = draw_doc_ids(jax.random.fold_in(splits[9], 71), 0)
    out_grad = centred(splits[8], (NSEQ, LEN, D), 1.0, 6.0, ((1, 32),))
    return dict(hidden_in=hidden_in, norm1_gain=norm1_gain, qkv_weight=qkv_weight, attn_weight=attn_weight, norm2_gain=norm2_gain, ffn_in_weight=ffn_in_weight, ffn_out_weight=ffn_out_weight, doc_ids=doc_ids, out_grad=out_grad)


neg_fill = -1e+30
theta_log = math.log(160000.0)
highest = lax.Precision.HIGHEST

@jax.custom_vjp
def low(v):
    return lax.optimization_barrier(v.astype(jnp.bfloat16)).astype(jnp.float32)

@jax.custom_vjp
def low_back(v):
    return v

def low_keep(v):
    return (low(v), None)

def low_pass(kept, grad):
    return (grad,)

def back_keep(v):
    return (v, None)

def back_low(kept, grad):
    return (low(grad),)
low.defvjp(low_keep, low_pass)
low_back.defvjp(back_keep, back_low)

def rope_tables(positions, width):
    freqs = jnp.exp(-(2.0 * jnp.arange(width // 2, dtype=jnp.float32) / width) * theta_log)
    angles = positions.astype(jnp.float32)[:, None] * freqs[None, :]
    angles = jnp.concatenate([angles, angles], axis=1)
    return (jnp.cos(angles), jnp.sin(angles))

def rotate(values, cosine, sine):
    half = values.shape[-1] // 2
    turned = jnp.concatenate([-values[..., half:], values[..., :half]], axis=-1)
    return values * cosine[:, None, :] + turned * sine[:, None, :]

def layer_norm(rows, gain):
    mean = lax.optimization_barrier(jnp.mean(rows, axis=-1, keepdims=True))
    cent = rows - mean
    var = lax.optimization_barrier(jnp.mean(cent * cent, axis=-1, keepdims=True))
    return cent * lax.rsqrt(var + 1e-05) * gain

def attention(query, keys, values, seg):
    length = query.shape[0]
    block = min(512, length)
    query_blocks = query.reshape(length // block, block, HEADS, HD)
    seg_blocks = seg.reshape(length // block, block)
    scale = 1.0 / math.sqrt(HD)

    def one_block(item):
        qblk, sblk = item
        scores = low_back(jnp.einsum('qhe,khe->hqk', qblk, keys, precision=highest) * scale)
        masked = jnp.where(sblk[None, :, None] == seg[None, None, :], scores, neg_fill)
        shifted = jnp.exp(masked - lax.optimization_barrier(jnp.max(masked, axis=-1, keepdims=True)))
        probs = low(shifted / lax.optimization_barrier(jnp.sum(shifted, axis=-1, keepdims=True)))
        return jnp.einsum('hqk,khe->qhe', probs, values, precision=highest)
    result = lax.map(jax.checkpoint(one_block), (query_blocks, seg_blocks))
    return result.reshape(length, HEADS, HD)

def layer(rows, seg, cosine, sine, gain1, wqkv, wattn, gain2, win, wout):
    length = rows.shape[0]
    normed1 = low(layer_norm(rows, gain1))
    qkv = low_back(jnp.einsum('ld,dthe->lthe', normed1, wqkv, precision=highest))
    query = low(rotate(qkv[:, 0], cosine, sine))
    keys = low(rotate(qkv[:, 1], cosine, sine))
    values = low(qkv[:, 2])
    attn = low(low_back(attention(query, keys, values, seg))).reshape(length, HEADS * HD)
    mid = rows + low_back(jnp.dot(attn, wattn.reshape(HEADS * HD, D), precision=highest))
    normed2 = low(layer_norm(mid, gain2))
    upper = low_back(jnp.einsum('ld,dgf->lgf', normed2, win, precision=highest))
    act = low(jax.nn.gelu(upper[:, 0], approximate=False) * upper[:, 1])
    return mid + jnp.dot(act, wout, precision=highest)

def reference(hidden_in, norm1_gain, qkv_weight, attn_weight, norm2_gain, ffn_in_weight, ffn_out_weight, doc_ids, out_grad):
    weights = tuple((w.astype(jnp.float32) for w in (norm1_gain, qkv_weight, attn_weight, norm2_gain, ffn_in_weight, ffn_out_weight)))
    cosine, sine = rope_tables(jnp.arange(LEN, dtype=jnp.int32), HD)

    def one_seq(totals, item):
        rows, seg, cot = item
        result, pull = jax.vjp(lambda r, *w: layer(r, seg, cosine, sine, *w), rows, *weights)
        grads = pull(cot)
        return (tuple((t + g for t, g in zip(totals, grads[1:]))), (result, grads[0]))
    zeros = tuple((jnp.zeros_like(w) for w in weights))
    totals, (outputs, in_grads) = lax.scan(one_seq, zeros, (hidden_in.astype(jnp.float32), doc_ids, out_grad.astype(jnp.float32)))
    return (outputs.astype(jnp.bfloat16), in_grads.astype(jnp.bfloat16), totals[0], totals[1], totals[2], totals[3], totals[4], totals[5])
```

```python
import functools
import math

import jax
import jax.numpy as jnp
from jax import lax
from jax.experimental import pallas as pl
from jax.experimental.pallas import tpu as pltpu
from jax.sharding import PartitionSpec as P

theta_log = math.log(160000.0)
neg_fill = -1e30
safe_bound = 60.0
log2_e = math.log2(math.e)
wide_keys = 1664
fine_keys = 512
cut_count = 4
bf16 = jnp.bfloat16
f32 = jnp.float32
vmem_limit = 56 * 2**20


def swap(block, axis, bits):
    size = lax.axis_size(axis)
    return lax.ppermute(block, axis, [(i, i ^ bits) for i in range(size)])


def bit_list(size):
    bits, b = [], 1
    while b < size:
        bits.append(b)
        b *= 2
    return bits


def total(value, axis):
    for b in bit_list(lax.axis_size(axis)):
        value = value + swap(value, axis, b)
    return value


def gather_blocks(block):
    held = {0: block}
    for b in reversed(bit_list(lax.axis_size("tp"))):
        for j in list(held):
            held[j ^ b] = swap(held[j], "tp", b)
    return [held[j] for j in range(len(held))]


def scatter_blocks(blocks):
    held = dict(enumerate(blocks))
    for b in bit_list(lax.axis_size("tp")):
        for j in sorted(held):
            if j & b:
                got = swap(held.pop(j), "tp", b)
                summed = held[j ^ b].astype(f32) + got.astype(f32)
                held[j ^ b] = summed if len(held) == 1 else summed.astype(bf16)
    return held[0]


def dot(a, b, ca, cb):
    return lax.dot_general(a, b, (((ca,), (cb,)), ((), ())), preferred_element_type=f32)


def lanes():
    return lax.broadcasted_iota(jnp.int32, (1, 128), 1)


def rot(u):
    first = (lanes() & 63) < 32
    return jnp.where(first, -pltpu.roll(u, 96, 1), pltpu.roll(u, 32, 1))


def rot_back(w):
    first = (lanes() & 63) < 32
    return jnp.where(first, pltpu.roll(w, 96, 1), -pltpu.roll(w, 32, 1))


def call(kernel, ins, outs, scratch, smem_ins=1, grid=None, in_specs=None, out_specs=None):
    whole = pl.BlockSpec(memory_space=pltpu.VMEM)
    if in_specs is None:
        in_specs = [pl.BlockSpec(memory_space=pltpu.SMEM)] * smem_ins + [whole] * (
            len(ins) - smem_ins
        )
        out_specs = [whole] * len(outs)
    extra = {} if grid is None else {"grid": grid}
    return pl.pallas_call(
        kernel,
        in_specs=in_specs,
        out_specs=out_specs,
        out_shape=outs,
        scratch_shapes=scratch,
        compiler_params=pltpu.CompilerParams(vmem_limit_bytes=vmem_limit),
        **extra,
    )(*ins)


def assemble(meta, pieces, x_scr):
    part = pieces[0].shape[0]
    for j, piece in enumerate(pieces):
        at = pl.multiple_of((meta[2] ^ j) * part, 8)
        x_scr[pl.ds(at, part), :] = piece[...].astype(f32)


def disperse(meta, x_scr, pieces):
    part = pieces[0].shape[0]
    for j, piece in enumerate(pieces):
        at = pl.multiple_of((meta[2] ^ j) * part, 8)
        piece[...] = x_scr[pl.ds(at, part), :].astype(bf16)


def qkv_kernel(heads, tp, half, scale, meta, *refs):
    pieces, refs = refs[:tp], refs[tp:]
    weight, ck, sk, cd, sd, x_ref, *refs = refs
    kv_outs, q_outs, (x_scr, kv_scr, q_scr) = refs[:heads], refs[heads : 2 * heads], refs[-3:]
    assemble(meta, pieces, x_scr)
    x = x_scr[...].astype(bf16)
    x_ref[...] = x
    left = lanes() < 64
    for h in range(heads):
        both = dot(x, weight[:, h * 256 : (h + 1) * 256], 1, 0)
        kv = both[:, :128]
        q = both[:, 128:]
        kv_scr[h] = (kv * ck[...] + rot(kv) * sk[...]).astype(bf16)
        q = (q * cd[...] + rot(q) * sd[...]) * scale
        q_scr[h] = jnp.where(left, q[:half], q[half:]).astype(bf16)
    for kh in range(heads):
        kv_outs[kh][...] = kv_scr[meta[1] ^ kh]
        q_outs[kh][...] = q_scr[meta[1] ^ kh]


def row_range(tok, meta, length):
    low = jnp.zeros_like(tok)
    high = jnp.full_like(tok, length)
    for d in range(cut_count):
        c = meta[3 + d]
        low = jnp.where(tok >= c, jnp.maximum(low, c), low)
        high = jnp.where(tok < c, jnp.minimum(high, c), high)
    return low, high


def load_keys(meta, ctx, rows, kv_refs, kvs, vx, sems):
    copies = []
    for k in range(ctx):
        at = pl.multiple_of((meta[0] ^ k) * rows, rows)
        copies.append(pltpu.make_async_copy(kv_refs[k], kvs.at[pl.ds(at, rows)], sems.at[k]))
    for c in copies:
        c.start()
    for c in copies:
        c.wait()
    vx[...] = jnp.where(lanes() < 64, jnp.ones((), bf16), kvs[...])


def attn_fwd_kernel(heads, ctx, rows, length, meta, *refs):
    q_refs, refs = refs[:heads], refs[heads:]
    kv_refs, refs = refs[:ctx], refs[ctx:]
    o_refs, refs = refs[:heads], refs[heads:]
    linv_ref, m_ref, kvs, vx, q_scr, qc, acc, m_scr, norms, sems = refs
    half = rows // 2
    i = pl.program_id(0)
    left = lanes() < 64

    @pl.when(i == 0)
    def _():
        load_keys(meta, ctx, rows, kv_refs, kvs, vx, sems)
        k = jnp.where(left, kvs[...].astype(f32), 0.0)
        norms[0] = jnp.max(jnp.sum(k * k, axis=1, keepdims=True))
        for c in range(heads):
            q_scr[c] = q_refs[c][...]

    q = q_scr[i].astype(f32)
    qa = jnp.where(left, q, 0.0)
    qb = jnp.where(left, pltpu.roll(q, 64, 1), 0.0)
    qc[:half] = qa.astype(bf16)
    qc[half:] = qb.astype(bf16)
    q_norm = jnp.max(jnp.sum(jnp.maximum(qa * qa, qb * qb), axis=1, keepdims=True))
    safe = q_norm * norms[0] < safe_bound * safe_bound
    single = meta[3] >= length
    fast = jnp.logical_and(safe, single)
    acc[...] = jnp.zeros_like(acc)
    m_scr[...] = jnp.zeros_like(m_scr)

    @pl.when(fast)
    def _():
        def step(j, _):
            keys = pl.ds(pl.multiple_of(j * wide_keys, wide_keys), wide_keys)
            e = jnp.exp2(dot(qc[...], kvs[keys, :], 1, 1)).astype(bf16)
            acc[...] += dot(e, vx[keys, :], 1, 0)
            return 0

        lax.fori_loop(0, length // wide_keys, step, 0)

    @pl.when(jnp.logical_not(fast))
    def _():
        first = (meta[0] ^ (i * (ctx // heads))) * rows
        tok = first + lax.broadcasted_iota(jnp.int32, (rows, 1), 0)
        low, high = row_range(tok, meta, length)
        j_low = lax.div(row_range(first, meta, length)[0], fine_keys)
        j_high = lax.div(row_range(first + rows - 1, meta, length)[1] + fine_keys - 1, fine_keys)

        def masked(j):
            keys = pl.ds(pl.multiple_of(j * fine_keys, fine_keys), fine_keys)
            spot = j * fine_keys + lax.broadcasted_iota(jnp.int32, (1, fine_keys), 1)
            allowed = jnp.logical_and(spot >= low, spot < high)
            return keys, allowed, dot(qc[...], kvs[keys, :], 1, 1)

        @pl.when(jnp.logical_not(safe))
        def _():
            m_scr[...] = jnp.full_like(m_scr, neg_fill)

            def peak(j, _):
                _, allowed, s = masked(j)
                s = jnp.max(jnp.where(allowed, s, neg_fill), axis=1, keepdims=True)
                m_scr[...] = jnp.maximum(m_scr[...], s)
                return 0

            lax.fori_loop(j_low, j_high, peak, 0)

        def step(j, _):
            keys, allowed, s = masked(j)
            e = jnp.where(allowed, jnp.exp2(s - m_scr[:, 0:1]), 0.0).astype(bf16)
            acc[...] += dot(e, vx[keys, :], 1, 0)
            return 0

        lax.fori_loop(j_low, j_high, step, 0)

    a = acc[...]
    o = a / pltpu.roll(a, 64, 1)
    out = jnp.where(left, pltpu.roll(o[:half], 64, 1), o[half:]).astype(bf16)
    for c in range(heads):

        @pl.when(i == c)
        def _(c=c):
            o_refs[c][...] = out

    inv = 1.0 / a
    linv_ref[...] = jnp.where(left, inv[:half], pltpu.roll(inv[half:], 64, 1))
    m_ref[...] = jnp.where(left, m_scr[:half], m_scr[half:])


def attn_bwd_kernel(heads, ctx, rows, length, meta, *refs):
    q_refs, refs = refs[:heads], refs[heads:]
    do_refs, refs = refs[:heads], refs[heads:]
    o_refs, refs = refs[:heads], refs[heads:]
    linv_ref, m_ref, *refs = refs
    kv_refs, refs = refs[:ctx], refs[ctx:]
    dq_refs, refs = refs[:heads], refs[heads:]
    dkv_refs, refs = refs[:ctx], refs[ctx:]
    kvs, vx, q_scr, do_scr, o_scr, qc, dc, qt, dt, dq_acc, dkv_t, dkv_n, sems = refs
    half = rows // 2
    i = pl.program_id(0)
    lane = lanes()
    left = lane < 64

    @pl.when(i == 0)
    def _():
        load_keys(meta, ctx, rows, kv_refs, kvs, vx, sems)
        dkv_t[...] = jnp.zeros_like(dkv_t)
        for c in range(heads):
            q_scr[c] = q_refs[c][...]
            do_scr[c] = do_refs[c][...]
            o_scr[c] = o_refs[c][...]

    q = q_scr[i].astype(f32)
    do = do_scr[i].astype(f32) * linv_ref[...]
    prod = do * o_scr[i].astype(f32)
    delta_a = jnp.sum(jnp.where(left, prod, 0.0), axis=1, keepdims=True)
    delta_b = jnp.sum(jnp.where(left, 0.0, prod), axis=1, keepdims=True)

    def extended(x, delta):
        coarse = delta.astype(bf16).astype(f32)
        ends = jnp.where(lane == 0, -coarse, jnp.where(lane == 1, coarse - delta, 0.0))
        return jnp.where(left, ends, x).astype(bf16)

    qc[:half] = jnp.where(left, q, 0.0).astype(bf16)
    qc[half:] = jnp.where(left, pltpu.roll(q, 64, 1), 0.0).astype(bf16)
    dc[:half] = extended(pltpu.roll(do, 64, 1), delta_a)
    dc[half:] = extended(do, delta_b)
    qt[...] = qc[...].astype(f32).T[:64].astype(bf16)
    dt[...] = dc[...].astype(f32).T[64:].astype(bf16)
    dq_acc[...] = jnp.zeros_like(dq_acc)
    shift = m_ref[...]
    shifted = jnp.max(jnp.abs(shift)) > 0.0
    single = meta[3] >= length
    fast = jnp.logical_and(single, jnp.logical_not(shifted))

    def accumulate(keys, e, allowed):
        ds = e * dot(dc[...], vx[keys, :], 1, 1)
        if allowed is not None:
            ds = jnp.where(allowed, ds, 0.0)
        ds = ds.astype(bf16)
        e = e.astype(bf16)
        dq_acc[...] += dot(ds, kvs[keys, :], 1, 0)
        dkv_t[:64, keys] += dot(qt[...], ds, 1, 0)
        dkv_t[64:, keys] += dot(dt[...], e, 1, 0)

    @pl.when(fast)
    def _():
        def step(j, _):
            keys = pl.ds(pl.multiple_of(j * wide_keys, wide_keys), wide_keys)
            accumulate(keys, jnp.exp2(dot(qc[...], kvs[keys, :], 1, 1)), None)
            return 0

        lax.fori_loop(0, length // wide_keys, step, 0)

    @pl.when(jnp.logical_not(fast))
    def _():
        first = (meta[0] ^ (i * (ctx // heads))) * rows
        tok = first + lax.broadcasted_iota(jnp.int32, (rows, 1), 0)
        low, high = row_range(tok, meta, length)
        j_low = lax.div(row_range(first, meta, length)[0], fine_keys)
        j_high = lax.div(row_range(first + rows - 1, meta, length)[1] + fine_keys - 1, fine_keys)
        m = jnp.concatenate([shift[:, 0:1], shift[:, 64:65]], axis=0)

        def step(j, _):
            keys = pl.ds(pl.multiple_of(j * fine_keys, fine_keys), fine_keys)
            spot = j * fine_keys + lax.broadcasted_iota(jnp.int32, (1, fine_keys), 1)
            allowed = jnp.logical_and(spot >= low, spot < high)
            s = dot(qc[...], kvs[keys, :], 1, 1)
            e = jnp.where(allowed, jnp.exp2(s - m), 0.0)
            accumulate(keys, e, allowed)
            return 0

        lax.fori_loop(j_low, j_high, step, 0)

    a = dq_acc[...] * 0.125
    out = jnp.where(left, a[:half], pltpu.roll(a[half:], 64, 1)).astype(bf16)
    for c in range(heads):

        @pl.when(i == c)
        def _(c=c):
            dq_refs[c][...] = out

    @pl.when(i == heads - 1)
    def _():
        is_key = lax.broadcasted_iota(jnp.int32, (128, 1), 0) < 64
        for j in range(length // wide_keys):
            part = dkv_t[:, j * wide_keys : (j + 1) * wide_keys]
            part = jnp.where(is_key, part * math.log(2.0), part)
            dkv_n[j * wide_keys : (j + 1) * wide_keys, :] = part.T.astype(bf16)
        copies = []
        for k in range(ctx):
            at = pl.multiple_of((meta[0] ^ k) * rows, rows)
            copies.append(
                pltpu.make_async_copy(dkv_n.at[pl.ds(at, rows)], dkv_refs[k], sems.at[k])
            )
        for c in copies:
            c.start()
        for c in copies:
            c.wait()


def proj_kernel(heads, tp, meta, *refs):
    o_refs, refs = refs[:heads], refs[heads:]
    weight, o_nat, *refs = refs
    pieces, (o_scr, x_scr) = refs[:tp], refs[tp:]
    half = o_refs[0].shape[0]
    left = lanes() < 64
    for kh in range(heads):
        o_scr[meta[1] ^ kh] = o_refs[kh][...]
    zero = jnp.zeros((), bf16)
    for h in range(heads):
        o = o_scr[h]
        o_nat[:half, h * 128 : (h + 1) * 128] = jnp.where(left, o, zero)
        o_nat[half:, h * 128 : (h + 1) * 128] = jnp.where(left, zero, o)
    x_scr[...] = dot(o_nat[...], weight[...], 1, 0)
    disperse(meta, x_scr, pieces)


def d_attn_kernel(heads, tp, meta, *refs):
    pieces, refs = refs[:tp], refs[tp:]
    weight, full, *refs = refs
    outs, (x_scr, d_scr) = refs[:heads], refs[heads:]
    half = outs[0].shape[0]
    left = lanes() < 64
    assemble(meta, pieces, x_scr)
    x = x_scr[...].astype(bf16)
    full[...] = x
    for h in range(heads):
        d = dot(x, weight[h * 128 : (h + 1) * 128, :], 1, 1)
        d_scr[h] = jnp.where(left, d[:half], d[half:]).astype(bf16)
    for kh in range(heads):
        outs[kh][...] = d_scr[meta[1] ^ kh]


def d_qkv_kernel(heads, ctx, tp, meta, *refs):
    dkv_refs, refs = refs[:ctx], refs[ctx:]
    dq_refs, refs = refs[:heads], refs[heads:]
    weight, ck, sk, cd, sd, d_all, *refs = refs
    pieces, (kv_scr, q_scr, x_scr) = refs[:tp], refs[tp:]
    half = dq_refs[0].shape[0]
    parts = ctx // heads
    left = lanes() < 64
    for kh in range(heads):
        z = dkv_refs[kh * parts][...].astype(f32)
        for kp in range(1, parts):
            z = z + dkv_refs[kh * parts + kp][...].astype(f32)
        kv_scr[meta[1] ^ kh] = (z * ck[...] + rot_back(z * sk[...])).astype(bf16)
        q_scr[meta[1] ^ kh] = dq_refs[kh][...]
    for h in range(heads):
        d_all[:, h * 256 : h * 256 + 128] = kv_scr[h]
        d = q_scr[h].astype(f32)
        d = jnp.concatenate([jnp.where(left, d, 0.0), jnp.where(left, 0.0, d)], axis=0)
        d = d * cd[...] + rot_back(d * sd[...])
        d_all[:, h * 256 + 128 : (h + 1) * 256] = d.astype(bf16)
    x_scr[...] = dot(d_all[...], weight[...], 1, 1)
    disperse(meta, x_scr, pieces)


def rope_tables(positions, width):
    freqs = jnp.exp(-(2.0 * jnp.arange(width // 2, dtype=f32) / width) * theta_log)
    angles = positions.astype(f32)[:, None] * freqs[None, :]
    cosine, sine = jnp.cos(angles), jnp.sin(angles)
    one, none = jnp.ones_like(angles), jnp.zeros_like(angles)
    lay = lambda *parts: jnp.concatenate(parts, axis=1)
    return (
        lay(cosine, cosine, one, one),
        lay(sine, sine, none, none),
        lay(cosine, cosine, cosine, cosine),
        lay(sine, sine, sine, sine),
    )


def layer_norm(rows, gain):
    mean = jnp.mean(rows, axis=-1, keepdims=True)
    cent = rows - mean
    var = jnp.mean(cent * cent, axis=-1, keepdims=True)
    return cent * lax.rsqrt(var + 1e-05) * gain


def shards(
    hidden_in,
    norm1_gain,
    qkv_weight,
    attn_weight,
    norm2_gain,
    ffn_in_weight,
    ffn_out_weight,
    doc_ids,
    out_grad,
):
    seqs = hidden_in.shape[0]
    width = hidden_in.shape[2]
    heads = qkv_weight.shape[2]
    head_dim = qkv_weight.shape[3]
    rows = doc_ids.shape[1]
    half = rows // 2
    ff = ffn_out_weight.shape[0]
    ctx, tp = lax.axis_size("ctx"), lax.axis_size("tp")
    parts = ctx // heads
    length = ctx * rows
    own = rows // tp
    me, spot = lax.axis_index("ctx"), lax.axis_index("tp")
    sds = jax.ShapeDtypeStruct

    steps = jnp.arange(1, cut_count + 1, dtype=jnp.int32)
    counts = jnp.sum((doc_ids[:, :, None] < steps).astype(f32), axis=1)
    cuts = total(counts, "ctx").astype(jnp.int32)
    place = jnp.stack([me, me // parts, spot]).astype(jnp.int32)
    metas = [jnp.concatenate([place, cuts[s]]) for s in range(seqs)]

    wq, wk, wv = qkv_weight[:, 0], qkv_weight[:, 1], qkv_weight[:, 2]
    w_all = jnp.concatenate([wk, wv, wq, wq], axis=2).reshape(width, heads * 256)
    w_out = jnp.concatenate([attn_weight, attn_weight], axis=1).reshape(heads * 128, width)
    w_in = ffn_in_weight.reshape(width, 2 * ff)
    tables = rope_tables(me * rows + jnp.arange(rows, dtype=jnp.int32), head_dim)
    scale = log2_e / math.sqrt(head_dim)

    resid = [hidden_in[s].astype(f32) for s in range(seqs)]
    full1, q_got, kv_got = [], [], []
    for s in range(seqs):
        blocks = gather_blocks(layer_norm(resid[s], norm1_gain).astype(bf16))
        outs = call(
            functools.partial(qkv_kernel, heads, tp, half, scale),
            [metas[s], *blocks, w_all, *tables],
            [sds((rows, width), bf16)]
            + [sds((rows, 128), bf16)] * heads
            + [sds((half, 128), bf16)] * heads,
            [
                pltpu.VMEM((rows, width), f32),
                pltpu.VMEM((heads, rows, 128), bf16),
                pltpu.VMEM((heads, half, 128), bf16),
            ],
        )
        full1.append(outs[0])
        kv, q = outs[1 : 1 + heads], outs[1 + heads :]
        q_got.append([q[0]] + [swap(q[h], "ctx", h * parts) for h in range(1, heads)])
        kv_got.append(
            [kv[0]] + [swap(kv[k // parts], "ctx", k) for k in range(1, ctx)]
        )

    smem = pl.BlockSpec(memory_space=pltpu.SMEM)
    hbm = pl.BlockSpec(memory_space=pl.ANY)
    small = pl.BlockSpec((half, 128), lambda i: (0, 0))
    tile = pl.BlockSpec((half, 128), lambda i: (i, 0))
    o_mine, linv, shift, o_nat, mid, grads_full = [], [], [], [], [], []
    for s in range(seqs):
        outs = call(
            functools.partial(attn_fwd_kernel, heads, ctx, rows, length),
            [metas[s], *q_got[s], *kv_got[s]],
            [sds((half, 128), bf16)] * heads + [sds((heads * half, 128), f32)] * 2,
            [
                pltpu.VMEM((length, 128), bf16),
                pltpu.VMEM((length, 128), bf16),
                pltpu.VMEM((heads, half, 128), bf16),
                pltpu.VMEM((rows, 128), bf16),
                pltpu.VMEM((rows, 128), f32),
                pltpu.VMEM((rows, 128), f32),
                pltpu.SMEM((1,), f32),
                pltpu.SemaphoreType.DMA((ctx,)),
            ],
            grid=(heads,),
            in_specs=[smem] + [small] * heads + [hbm] * ctx,
            out_specs=[small] * heads + [tile, tile],
        )
        o_mine.append(outs[:heads])
        linv.append(outs[heads])
        shift.append(outs[heads + 1])
        back = [outs[0]] + [swap(outs[h], "ctx", h * parts) for h in range(1, heads)]
        outs = call(
            functools.partial(proj_kernel, heads, tp),
            [metas[s], *back, w_out],
            [sds((rows, heads * 128), bf16)] + [sds((own, width), bf16)] * tp,
            [pltpu.VMEM((heads, half, 128), bf16), pltpu.VMEM((rows, width), f32)],
        )
        o_nat.append(outs[0])
        mid.append(resid[s] + scatter_blocks(outs[1:]))
        grads_full.append(jnp.concatenate(gather_blocks(out_grad[s]), axis=0))

    block_out, d_mid, dmid_full, d_attn, gain2 = [], [], [], [], 0.0
    g_out_w, g_in_w, g_attn_w = 0.0, 0.0, 0.0
    for s in range(seqs):
        normed2, pull_norm2 = jax.vjp(layer_norm, mid[s], norm2_gain)
        full2 = jnp.concatenate(gather_blocks(normed2.astype(bf16)), axis=0)
        upper = dot(full2, w_in, 1, 0)
        first, second = upper[:, :ff], upper[:, ff:]
        gated, pull_gelu = jax.vjp(
            lambda a, b: jax.nn.gelu(a, approximate=False) * b, first, second
        )
        act = gated.astype(bf16)
        d_act = dot(grads_full[s], ffn_out_weight, 1, 1)
        d_upper = jnp.concatenate(pull_gelu(d_act), axis=1).astype(bf16)
        d_part = dot(d_upper, w_in, 1, 1).astype(bf16)
        d_normed2 = scatter_blocks([d_part[j * own : (j + 1) * own] for j in range(tp)])
        d_mid_norm, d_gain = pull_norm2(d_normed2)
        gain2 = gain2 + d_gain
        d_mid.append(out_grad[s].astype(f32) + d_mid_norm)
        pieces = gather_blocks(d_mid[s].astype(bf16))
        outs = call(
            functools.partial(d_attn_kernel, heads, tp),
            [metas[s], *pieces, w_out],
            [sds((rows, width), bf16)] + [sds((half, 128), bf16)] * heads,
            [pltpu.VMEM((rows, width), f32), pltpu.VMEM((heads, half, 128), bf16)],
        )
        dmid_full.append(outs[0])
        d = outs[1:]
        d_attn.append([d[0]] + [swap(d[h], "ctx", h * parts) for h in range(1, heads)])
        out_part = dot(act, ffn_out_weight, 1, 0).astype(bf16)
        ffn_sum = scatter_blocks([out_part[j * own : (j + 1) * own] for j in range(tp)])
        block_out.append((mid[s] + ffn_sum).astype(bf16))
        g_out_w = g_out_w + dot(act, grads_full[s], 0, 0)
        g_in_w = g_in_w + dot(full2, d_upper, 0, 0)
        g_attn_w = g_attn_w + dot(o_nat[s], dmid_full[s], 0, 0)
    g_attn_w = jnp.sum(g_attn_w.reshape(heads, 2, head_dim, width), axis=1)
    early = [lax.psum(g.astype(bf16), "ctx").astype(f32) for g in (g_out_w, g_in_w, g_attn_w)]

    d_all, in_grad, gain1 = [], [], 0.0
    for s in range(seqs):
        outs = call(
            functools.partial(attn_bwd_kernel, heads, ctx, rows, length),
            [metas[s], *q_got[s], *d_attn[s], *o_mine[s], linv[s], shift[s], *kv_got[s]],
            [sds((half, 128), bf16)] * heads + [sds((rows, 128), bf16)] * ctx,
            [
                pltpu.VMEM((length, 128), bf16),
                pltpu.VMEM((length, 128), bf16),
                pltpu.VMEM((heads, half, 128), bf16),
                pltpu.VMEM((heads, half, 128), bf16),
                pltpu.VMEM((heads, half, 128), bf16),
                pltpu.VMEM((rows, 128), bf16),
                pltpu.VMEM((rows, 128), bf16),
                pltpu.VMEM((64, rows), bf16),
                pltpu.VMEM((64, rows), bf16),
                pltpu.VMEM((rows, 128), f32),
                pltpu.VMEM((128, length), f32),
                pltpu.VMEM((length, 128), bf16),
                pltpu.SemaphoreType.DMA((ctx,)),
            ],
            grid=(heads,),
            in_specs=[smem] + [small] * (3 * heads) + [tile, tile] + [hbm] * ctx,
            out_specs=[small] * heads + [hbm] * ctx,
        )
        dq = [outs[0]] + [swap(outs[h], "ctx", h * parts) for h in range(1, heads)]
        dkv = outs[heads:]
        dkv = [dkv[0]] + [swap(dkv[k], "ctx", k) for k in range(1, ctx)]
        outs = call(
            functools.partial(d_qkv_kernel, heads, ctx, tp),
            [metas[s], *dkv, *dq, w_all, *tables],
            [sds((rows, heads * 256), bf16)] + [sds((own, width), bf16)] * tp,
            [
                pltpu.VMEM((heads, rows, 128), bf16),
                pltpu.VMEM((heads, half, 128), bf16),
                pltpu.VMEM((rows, width), f32),
            ],
        )
        d_all.append(outs[0])
        _, pull_norm1 = jax.vjp(layer_norm, resid[s], norm1_gain)
        d_in_norm, d_gain = pull_norm1(scatter_blocks(outs[1:]))
        gain1 = gain1 + d_gain
        in_grad.append((d_mid[s] + d_in_norm).astype(bf16))
    g_qkv_w = sum(dot(full1[s], d_all[s], 0, 0) for s in range(seqs))
    g_qkv_w = g_qkv_w.reshape(width, heads, 4, head_dim)
    g_qkv_w = jnp.stack(
        [g_qkv_w[:, :, 2] + g_qkv_w[:, :, 3], g_qkv_w[:, :, 0], g_qkv_w[:, :, 1]], axis=1
    )
    g_qkv_w = lax.psum(g_qkv_w.astype(bf16), "ctx").astype(f32)
    gains = total(total(jnp.stack([gain1, gain2]), "tp"), "ctx")
    return (
        jnp.stack(block_out),
        jnp.stack(in_grad),
        gains[0],
        g_qkv_w,
        early[2],
        gains[1],
        early[1].reshape(width, 2, ff),
        early[0],
    )


def solution(mesh):
    in_specs = (
        P(None, ("ctx", "tp"), None),
        P(),
        P(None, None, "tp", None),
        P("tp", None, None),
        P(),
        P(None, None, "tp"),
        P("tp", None),
        P(None, "ctx"),
        P(None, ("ctx", "tp"), None),
    )
    out_specs = (
        P(None, ("ctx", "tp"), None),
        P(None, ("ctx", "tp"), None),
        P(),
        P(None, None, "tp", None),
        P("tp", None, None),
        P(),
        P(None, None, "tp"),
        P("tp", None),
    )
    return jax.shard_map(shards, mesh=mesh, in_specs=in_specs, out_specs=out_specs, check_vma=False)
```

```python
import functools
import math

import jax
import jax.numpy as jnp
from jax import lax
from jax.experimental import pallas as pl
from jax.experimental.pallas import tpu as pltpu
from jax.sharding import PartitionSpec as P

theta_log = math.log(160000.0)
neg_fill = -1e30
safe_bound = 60.0
log2_e = math.log2(math.e)
wide_keys = 1664
fine_keys = 512
cut_count = 4
bf16 = jnp.bfloat16
f32 = jnp.float32
vmem_limit = 56 * 2**20


def swap(block, axis, bits):
    size = lax.axis_size(axis)
    return lax.ppermute(block, axis, [(i, i ^ bits) for i in range(size)])


def bit_list(size):
    bits, b = [], 1
    while b < size:
        bits.append(b)
        b *= 2
    return bits


def total(value, axis):
    for b in bit_list(lax.axis_size(axis)):
        value = value + swap(value, axis, b)
    return value


def gather_blocks(block, axis="tp", bits=None):
    held = {0: block}
    for b in reversed(bit_list(lax.axis_size(axis)) if bits is None else bits):
        for j in list(held):
            held[j ^ b] = swap(held[j], axis, b)
    return [held[j] for j in sorted(held)]


def scatter_blocks(blocks, axis="tp", notes=None):
    held = dict(blocks)
    for b in bit_list(max(held) + 1):
        for j in sorted(held):
            if j & b:
                got = swap(held.pop(j), axis, b)
                summed = held[j ^ b].astype(f32) + got.astype(f32)
                held[j ^ b] = summed if len(held) == 1 else summed.astype(bf16)
        if notes is not None:
            notes.append(list(held.values()))
    return held[0]


def row_order(size, turn):
    bits = bit_list(size)
    bits = bits[turn:] + bits[:turn]
    return bits, sorted(range(size), key=lambda k: [k & b for b in bits])


def sum_halves(keep, send, axis, bits):
    for n, b in enumerate(bits):
        held = (keep.astype(f32) + swap(send, axis, b).astype(f32)).astype(bf16)
        if n < len(bits) - 1:
            mid = held.shape[0] // 2
            keep, send = held[:mid], held[mid:]
    for b in reversed(bits[1:]):
        held = jnp.concatenate([held, swap(held, axis, b)], axis=0)
    return held, swap(held, axis, bits[0])


def dot(a, b, ca, cb):
    return lax.dot_general(a, b, (((ca,), (cb,)), ((), ())), preferred_element_type=f32)


def lanes():
    return lax.broadcasted_iota(jnp.int32, (1, 128), 1)


def rot(u):
    first = (lanes() & 63) < 32
    return jnp.where(first, -pltpu.roll(u, 96, 1), pltpu.roll(u, 32, 1))


def rot_back(w):
    first = (lanes() & 63) < 32
    return jnp.where(first, pltpu.roll(w, 96, 1), -pltpu.roll(w, 32, 1))


def call(
    kernel,
    ins,
    outs,
    scratch,
    cost,
    smem_ins=1,
    grid=None,
    in_specs=None,
    out_specs=None,
    deps=(),
):
    whole = pl.BlockSpec(memory_space=pltpu.VMEM)
    if in_specs is None:
        in_specs = [pl.BlockSpec(memory_space=pltpu.SMEM)] * smem_ins + [whole] * (
            len(ins) - smem_ins
        )
        out_specs = [whole] * len(outs)
    extra = {} if grid is None else {"grid": grid}
    moved = sum(a.size * a.dtype.itemsize for a in [*ins, *outs])
    time = int(cost * 1.15e9)
    used = len(ins)
    ins = [*ins, *deps]
    in_specs = in_specs + [pl.BlockSpec(memory_space=pl.ANY)] * len(deps)

    def body(*refs):
        kernel(*refs[:used], *refs[len(ins) :])

    return pl.pallas_call(
        body,
        in_specs=in_specs,
        out_specs=out_specs,
        out_shape=outs,
        scratch_shapes=scratch,
        compiler_params=pltpu.CompilerParams(vmem_limit_bytes=vmem_limit),
        cost_estimate=pl.CostEstimate(
            flops=time, transcendentals=0, bytes_accessed=int(moved)
        ),
        **extra,
    )(*ins)


def assemble(meta, pieces, x_scr):
    part = pieces[0].shape[0]
    for j, piece in enumerate(pieces):
        at = pl.multiple_of((meta[2] ^ j) * part, 8)
        x_scr[pl.ds(at, part), :] = piece[...].astype(f32)


def disperse(meta, x_scr, pieces):
    part = pieces[0].shape[0]
    for j, piece in enumerate(pieces):
        at = pl.multiple_of((meta[2] ^ j) * part, 8)
        piece[...] = x_scr[pl.ds(at, part), :].astype(bf16)


def pair(u, v):
    return jnp.where(lanes() < 64, u, pltpu.roll(v, 64, 1))


def pair_right(u, v):
    return jnp.where(lanes() < 64, pltpu.roll(u, 64, 1), v)


def qkv_kernel(heads, tp, half, scale, meta, *refs):
    pieces, refs = refs[:tp], refs[tp:]
    weight, cosine, sine, x_ref, *refs = refs
    outs, (x_scr, kv_scr, q_scr) = refs[:heads], refs[heads:]
    assemble(meta, pieces, x_scr)
    x = x_scr[...].astype(bf16)
    x_ref[...] = x
    every = heads * 64
    for t in range(heads // 2):
        q, k, v = [
            dot(x, weight[:, n * every + t * 128 : n * every + (t + 1) * 128], 1, 0)
            for n in range(3)
        ]
        q = (q * cosine[...] + rot(q) * sine[...]) * scale
        k = k * cosine[...] + rot(k) * sine[...]
        kv_scr[2 * t] = pair(k, v).astype(bf16)
        kv_scr[2 * t + 1] = pair_right(k, v).astype(bf16)
        q_scr[2 * t] = pair(q[:half], q[half:]).astype(bf16)
        q_scr[2 * t + 1] = pair_right(q[:half], q[half:]).astype(bf16)
    for kh in range(heads):
        outs[kh][: 2 * half, :] = kv_scr[meta[1] ^ kh]
        outs[kh][2 * half :, :] = q_scr[meta[1] ^ kh]


def row_range(tok, meta, length):
    low = jnp.zeros_like(tok)
    high = jnp.full_like(tok, length)
    for d in range(cut_count):
        c = meta[3 + d]
        low = jnp.where(tok >= c, jnp.maximum(low, c), low)
        high = jnp.where(tok < c, jnp.minimum(high, c), high)
    return low, high


def load_keys(meta, rows, plan, got, kvs, vx, q_scr, sems):
    heads = q_scr.shape[0]
    copies = []
    for c in range(heads):
        source = got[c].at[pl.ds(rows, rows // 2)]
        copies.append(pltpu.make_async_copy(source, q_scr.at[c], sems.at[c]))
    if plan is None:
        copies.append(pltpu.make_async_copy(got[heads], kvs, sems.at[heads]))
    else:
        for n, (ref, start, k) in enumerate(plan):
            at = pl.multiple_of((meta[0] ^ k) * rows, rows)
            source = got[ref].at[pl.ds(start, rows)]
            target = kvs.at[pl.ds(at, rows)]
            copies.append(pltpu.make_async_copy(source, target, sems.at[heads + n]))
    for c in copies:
        c.start()
    for c in copies:
        c.wait()
    vx[...] = jnp.where(lanes() < 64, jnp.ones((), bf16), kvs[...])


def attn_fwd_kernel(heads, ctx, rows, length, count, plan, chosen, meta, *refs):
    got, refs = refs[:count], refs[count:]
    o_refs, refs = refs[: len(chosen)], refs[len(chosen) :]
    linv_ref, m_ref, zero, kv_out, kvs, vx, q_scr, qc, acc, m_scr, norms, sems = refs
    half = rows // 2
    turn = pl.program_id(0)
    i = turn + chosen[0]
    left = lanes() < 64

    @pl.when(turn == 0)
    def _():
        zero[...] = jnp.zeros_like(zero)
        load_keys(meta, rows, plan, got, kvs, vx, q_scr, sems)
        if plan is not None:
            keep = pltpu.make_async_copy(kvs, kv_out, sems.at[0])
            keep.start()
        k = jnp.where(left, kvs[...].astype(f32), 0.0)
        norms[0] = jnp.max(jnp.sum(k * k, axis=1, keepdims=True))
        if plan is not None:
            keep.wait()

    q = q_scr[i].astype(f32)
    qa = jnp.where(left, q, 0.0)
    qb = jnp.where(left, pltpu.roll(q, 64, 1), 0.0)
    qc[:half] = qa.astype(bf16)
    qc[half:] = qb.astype(bf16)
    q_norm = jnp.max(jnp.sum(jnp.maximum(qa * qa, qb * qb), axis=1, keepdims=True))
    safe = q_norm * norms[0] < safe_bound * safe_bound
    single = meta[3] >= length
    fast = jnp.logical_and(safe, single)
    acc[...] = jnp.zeros_like(acc)
    m_scr[...] = jnp.zeros_like(m_scr)

    @pl.when(fast)
    def _():
        def step(j, _):
            keys = pl.ds(pl.multiple_of(j * wide_keys, wide_keys), wide_keys)
            e = jnp.exp2(dot(qc[...], kvs[keys, :], 1, 1)).astype(bf16)
            acc[...] += dot(e, vx[keys, :], 1, 0)
            return 0

        lax.fori_loop(0, length // wide_keys, step, 0)

    @pl.when(jnp.logical_not(fast))
    def _():
        first = (meta[0] ^ (i * (ctx // heads))) * rows
        tok = first + lax.broadcasted_iota(jnp.int32, (rows, 1), 0)
        low, high = row_range(tok, meta, length)
        j_low = lax.div(row_range(first, meta, length)[0], fine_keys)
        j_high = lax.div(row_range(first + rows - 1, meta, length)[1] + fine_keys - 1, fine_keys)

        def masked(j):
            keys = pl.ds(pl.multiple_of(j * fine_keys, fine_keys), fine_keys)
            spot = j * fine_keys + lax.broadcasted_iota(jnp.int32, (1, fine_keys), 1)
            allowed = jnp.logical_and(spot >= low, spot < high)
            return keys, allowed, dot(qc[...], kvs[keys, :], 1, 1)

        @pl.when(jnp.logical_not(safe))
        def _():
            m_scr[...] = jnp.full_like(m_scr, neg_fill)

            def peak(j, _):
                _, allowed, s = masked(j)
                s = jnp.max(jnp.where(allowed, s, neg_fill), axis=1, keepdims=True)
                m_scr[...] = jnp.maximum(m_scr[...], s)
                return 0

            lax.fori_loop(j_low, j_high, peak, 0)

        def step(j, _):
            keys, allowed, s = masked(j)
            e = jnp.where(allowed, jnp.exp2(s - m_scr[:, 0:1]), 0.0).astype(bf16)
            acc[...] += dot(e, vx[keys, :], 1, 0)
            return 0

        lax.fori_loop(j_low, j_high, step, 0)

    a = acc[...]
    o = a / pltpu.roll(a, 64, 1)
    out = jnp.where(left, pltpu.roll(o[:half], 64, 1), o[half:]).astype(bf16)
    for c in range(len(chosen)):

        @pl.when(turn == c)
        def _(c=c):
            o_refs[c][...] = out

    inv = 1.0 / a
    linv_ref[...] = jnp.where(left, inv[:half], pltpu.roll(inv[half:], 64, 1))
    m_ref[...] = jnp.where(left, m_scr[:half], m_scr[half:])


def attn_bwd_kernel(heads, ctx, rows, length, groups, meta, *refs):
    do_refs, refs = refs[:heads], refs[heads:]
    o_refs, refs = refs[:heads], refs[heads:]
    linv_refs, refs = refs[: len(groups)], refs[len(groups) :]
    m_refs, refs = refs[: len(groups)], refs[len(groups) :]
    got, refs = refs[: heads + 1], refs[heads + 1 :]
    dq_refs, refs = refs[:heads], refs[heads:]
    parts = ctx // heads
    dkv_refs, zero, refs = refs[:parts], refs[parts], refs[parts + 1 :]
    kvs, vx, q_scr, do_scr, o_scr, linv_scr, m_scr, *refs = refs
    qc, dc, qt, dt, dq_acc, dkv_t, dkv_n, sems = refs
    half = rows // 2
    i = pl.program_id(0)
    lane = lanes()
    left = lane < 64

    @pl.when(i == 0)
    def _():
        load_keys(meta, rows, None, got, kvs, vx, q_scr, sems)
        zero[...] = jnp.zeros_like(zero)
        dkv_t[...] = jnp.zeros_like(dkv_t)
        for c in range(heads):
            do_scr[c] = do_refs[c][...]
            o_scr[c] = o_refs[c][...]
        for n, g in enumerate(groups):
            side = slice(g[0] * half, (g[-1] + 1) * half)
            linv_scr[side, :] = linv_refs[n][...]
            m_scr[side, :] = m_refs[n][...]

    q = q_scr[i].astype(f32)
    here = pl.ds(pl.multiple_of(i * half, half), half)
    do = do_scr[i].astype(f32) * linv_scr[here, :]
    prod = do * o_scr[i].astype(f32)
    delta_a = jnp.sum(jnp.where(left, prod, 0.0), axis=1, keepdims=True)
    delta_b = jnp.sum(jnp.where(left, 0.0, prod), axis=1, keepdims=True)

    def extended(x, delta):
        coarse = delta.astype(bf16).astype(f32)
        ends = jnp.where(lane == 0, -coarse, jnp.where(lane == 1, coarse - delta, 0.0))
        return jnp.where(left, ends, x).astype(bf16)

    qc[:half] = jnp.where(left, q, 0.0).astype(bf16)
    qc[half:] = jnp.where(left, pltpu.roll(q, 64, 1), 0.0).astype(bf16)
    dc[:half] = extended(pltpu.roll(do, 64, 1), delta_a)
    dc[half:] = extended(do, delta_b)
    qt[...] = qc[...].astype(f32).T[:64].astype(bf16)
    dt[...] = dc[...].astype(f32).T[64:].astype(bf16)
    dq_acc[...] = jnp.zeros_like(dq_acc)
    shift = m_scr[here, :]
    shifted = jnp.max(jnp.abs(shift)) > 0.0
    single = meta[3] >= length
    fast = jnp.logical_and(single, jnp.logical_not(shifted))

    def accumulate(keys, e, allowed):
        ds = e * dot(dc[...], vx[keys, :], 1, 1)
        if allowed is not None:
            ds = jnp.where(allowed, ds, 0.0)
        ds = ds.astype(bf16)
        e = e.astype(bf16)
        dq_acc[...] += dot(ds, kvs[keys, :], 1, 0)
        dkv_t[:64, keys] += dot(qt[...], ds, 1, 0)
        dkv_t[64:, keys] += dot(dt[...], e, 1, 0)

    @pl.when(fast)
    def _():
        def step(j, _):
            keys = pl.ds(pl.multiple_of(j * wide_keys, wide_keys), wide_keys)
            accumulate(keys, jnp.exp2(dot(qc[...], kvs[keys, :], 1, 1)), None)
            return 0

        lax.fori_loop(0, length // wide_keys, step, 0)

    @pl.when(jnp.logical_not(fast))
    def _():
        first = (meta[0] ^ (i * (ctx // heads))) * rows
        tok = first + lax.broadcasted_iota(jnp.int32, (rows, 1), 0)
        low, high = row_range(tok, meta, length)
        j_low = lax.div(row_range(first, meta, length)[0], fine_keys)
        j_high = lax.div(row_range(first + rows - 1, meta, length)[1] + fine_keys - 1, fine_keys)
        m = jnp.concatenate([shift[:, 0:1], shift[:, 64:65]], axis=0)

        def step(j, _):
            keys = pl.ds(pl.multiple_of(j * fine_keys, fine_keys), fine_keys)
            spot = j * fine_keys + lax.broadcasted_iota(jnp.int32, (1, fine_keys), 1)
            allowed = jnp.logical_and(spot >= low, spot < high)
            s = dot(qc[...], kvs[keys, :], 1, 1)
            e = jnp.where(allowed, jnp.exp2(s - m), 0.0)
            accumulate(keys, e, allowed)
            return 0

        lax.fori_loop(j_low, j_high, step, 0)

    a = dq_acc[...] * 0.125
    out = jnp.where(left, a[:half], pltpu.roll(a[half:], 64, 1)).astype(bf16)
    for c in range(heads):

        @pl.when(i == c)
        def _(c=c):
            dq_refs[c][...] = out

    @pl.when(i == heads - 1)
    def _():
        is_key = lax.broadcasted_iota(jnp.int32, (128, 1), 0) < 64
        for j in range(length // wide_keys):
            part = dkv_t[:, j * wide_keys : (j + 1) * wide_keys]
            part = jnp.where(is_key, part * math.log(2.0), part)
            dkv_n[j * wide_keys : (j + 1) * wide_keys, :] = part.T.astype(bf16)
        copies = []
        for k in range(ctx):
            at = pl.multiple_of((meta[0] ^ k) * rows, rows)
            target = dkv_refs[k % parts].at[pl.ds(k // parts * rows, rows)]
            copies.append(pltpu.make_async_copy(dkv_n.at[pl.ds(at, rows)], target, sems.at[k]))
        for c in copies:
            c.start()
        for c in copies:
            c.wait()


def proj_kernel(heads, tp, meta, *refs):
    o_refs, refs = refs[:heads], refs[heads:]
    weight, o_nat, *refs = refs
    pieces, (o_scr, x_scr) = refs[:tp], refs[tp:]
    half = o_refs[0].shape[0]
    for kh in range(heads):
        o_scr[meta[1] ^ kh] = o_refs[kh][...]
    for t in range(heads // 2):
        u, v = o_scr[2 * t].astype(f32), o_scr[2 * t + 1].astype(f32)
        o_nat[:half, t * 128 : (t + 1) * 128] = pair(u, v).astype(bf16)
        o_nat[half:, t * 128 : (t + 1) * 128] = pair_right(u, v).astype(bf16)
    x_scr[...] = dot(o_nat[...], weight[...], 1, 0)
    disperse(meta, x_scr, pieces)


def d_attn_kernel(heads, tp, meta, *refs):
    pieces, refs = refs[:tp], refs[tp:]
    weight, full, *refs = refs
    outs, (x_scr, d_scr) = refs[:heads], refs[heads:]
    half = outs[0].shape[0]
    assemble(meta, pieces, x_scr)
    x = x_scr[...].astype(bf16)
    full[...] = x
    for t in range(heads // 2):
        d = dot(x, weight[t * 128 : (t + 1) * 128, :], 1, 1)
        d_scr[2 * t] = pair(d[:half], d[half:]).astype(bf16)
        d_scr[2 * t + 1] = pair_right(d[:half], d[half:]).astype(bf16)
    for kh in range(heads):
        outs[kh][...] = d_scr[meta[1] ^ kh]


def d_qkv_kernel(heads, tp, half, meta, *refs):
    got, refs = refs[:heads], refs[heads:]
    weight, cosine, sine, normed, d_all, gain, *refs = refs
    pieces, (scr, x_scr) = refs[:tp], refs[tp:]
    every = heads * 64
    for kh in range(heads):
        scr[meta[1] ^ kh] = got[kh][...]
    for t in range(heads // 2):
        u, v = scr[2 * t].astype(f32), scr[2 * t + 1].astype(f32)
        dk, dv = pair(u[: 2 * half], v[: 2 * half]), pair_right(u[: 2 * half], v[: 2 * half])
        u, v = u[2 * half :], v[2 * half :]
        dq = jnp.concatenate([pair(u, v), pair_right(u, v)], axis=0)
        dq = dq * cosine[...] + rot_back(dq * sine[...])
        dk = dk * cosine[...] + rot_back(dk * sine[...])
        for n, d in enumerate((dq, dk, dv)):
            d_all[:, n * every + t * 128 : n * every + (t + 1) * 128] = d.astype(bf16)
    x_scr[...] = dot(d_all[...], weight[...], 1, 1)
    gain[...] = jnp.sum(x_scr[...] * normed[...].astype(f32), axis=0, keepdims=True)
    disperse(meta, x_scr, pieces)


def deal_kernel(orders, meta, grad, *outs):
    part, wide = grad.shape[0] // len(orders[0]), outs[0].shape[1]
    deep = outs[0].shape[0] // part
    for c in range(grad.shape[1] // wide):
        for n, k in enumerate(orders[c]):
            at = pl.multiple_of((meta[0] ^ k) * part, part)
            out, place = outs[c * (len(orders[c]) // deep) + n // deep], n % deep * part
            out[place : place + part, :] = grad[
                pl.ds(at, part), c * wide : (c + 1) * wide
            ].astype(bf16)


def undeal_kernel(orders, count, meta, *refs):
    ins, outs = refs[:count], refs[count:]
    each = count // len(orders)
    for c, order in enumerate(orders):
        part = outs[0].shape[0] // len(order)
        deep = len(order) // each
        wide = ins[c * each].shape[1]
        for n, k in enumerate(order):
            at = pl.ds(pl.multiple_of((meta[0] ^ k) * part, part), part)
            place = n % deep * part
            block = ins[c * each + n // deep][place : place + part, :].astype(f32)
            first = c * wide
            for out in outs:
                size = min(out.shape[1], wide) if len(outs) > 1 else wide
                if len(outs) > 1:
                    out[at, :] = block[:, first : first + size]
                    first += size
                else:
                    out[at, first : first + wide] = block


def rope_tables(positions, width):
    freqs = jnp.exp(-(2.0 * jnp.arange(width // 2, dtype=f32) / width) * theta_log)
    angles = positions.astype(f32)[:, None] * freqs[None, :]
    cosine, sine = jnp.cos(angles), jnp.sin(angles)
    lay = lambda u: jnp.concatenate([u, u, u, u], axis=1)
    return lay(cosine), lay(sine)


def layer_norm(rows, gain):
    mean = jnp.mean(rows, axis=-1, keepdims=True)
    cent = rows - mean
    var = jnp.mean(cent * cent, axis=-1, keepdims=True)
    return cent * lax.rsqrt(var + 1e-05) * gain


def shards(
    hidden_in,
    norm1_gain,
    qkv_weight,
    attn_weight,
    norm2_gain,
    ffn_in_weight,
    ffn_out_weight,
    doc_ids,
    out_grad,
):
    seqs = hidden_in.shape[0]
    width = hidden_in.shape[2]
    heads = qkv_weight.shape[2]
    head_dim = qkv_weight.shape[3]
    rows = doc_ids.shape[1]
    half = rows // 2
    ff = ffn_out_weight.shape[0]
    ctx, tp = lax.axis_size("ctx"), lax.axis_size("tp")
    parts = ctx // heads
    length = ctx * rows
    own = rows // tp
    me, spot = lax.axis_index("ctx"), lax.axis_index("tp")
    sds = jax.ShapeDtypeStruct

    steps = jnp.arange(1, cut_count + 1, dtype=jnp.int32)
    counts = jnp.sum((doc_ids[:, :, None] < steps).astype(f32), axis=1)
    cuts = total(counts, "ctx").astype(jnp.int32)
    place = jnp.stack([me, me // parts, spot]).astype(jnp.int32)
    metas = [jnp.concatenate([place, cuts[s]]) for s in range(seqs)]

    every = heads * head_dim
    w_all = qkv_weight.reshape(width, 3 * every)
    w_out = attn_weight.reshape(every, width)
    w_in = ffn_in_weight.reshape(width, 2 * ff)
    tables = rope_tables(me * rows + jnp.arange(rows, dtype=jnp.int32), head_dim)
    scale = log2_e / math.sqrt(head_dim)

    resid = [hidden_in[s].astype(f32) for s in range(seqs)]
    full1, sents, mines = [], [], []

    def spread(s, zero):
        sent, mine = sents[s], mines[s]
        rest = jnp.concatenate([m[:rows] for m in mine[1:]], axis=0) + zero
        held = [(sent[0], [0]), (rest, [h * parts for h in range(1, heads)])]
        plan = [(h, 0, h * parts) for h in range(heads)]
        arrays = list(mine)
        for b in bit_list(parts):
            for block, ks in list(held):
                ks = [k ^ b for k in ks]
                held.append((swap(block, "ctx", b), ks))
                plan += [(len(arrays), n * rows, k) for n, k in enumerate(ks)]
                arrays.append(held[-1][0])
        return arrays, rest, plan

    for s in range(seqs):
        blocks = gather_blocks(layer_norm(resid[s], norm1_gain).astype(bf16))
        outs = call(
            functools.partial(qkv_kernel, heads, tp, half, scale),
            [place, *blocks, w_all, *tables],
            [sds((rows, width), bf16)] + [sds((rows + half, 128), bf16)] * heads,
            [
                pltpu.VMEM((rows, width), f32),
                pltpu.VMEM((heads, rows, 128), bf16),
                pltpu.VMEM((heads, half, 128), bf16),
            ],
            7,
            deps=[got[0][1]] if s else [cuts],
        )
        full1.append(outs[0])
        sent = outs[1:]
        sents.append(sent)
        mines.append([sent[0]] + [swap(sent[h], "ctx", h * parts) for h in range(1, heads)])
        if s == 0:
            got = [spread(0, jnp.zeros((), bf16))]

    smem = pl.BlockSpec(memory_space=pltpu.SMEM)
    hbm = pl.BlockSpec(memory_space=pl.ANY)
    small = pl.BlockSpec((half, 128), lambda i: (0, 0))
    tile = pl.BlockSpec((half, 128), lambda i: (i, 0))
    key_scratch = [
        pltpu.VMEM((length, 128), bf16),
        pltpu.VMEM((length, 128), bf16),
        pltpu.VMEM((heads, half, 128), bf16),
    ]
    sems = pltpu.SemaphoreType.DMA((ctx + heads,))

    def attend(s, chosen, deps):
        first = kept[s] is None
        ins = got[s][0] if first else [*mines[s], kept[s]]
        tiles = len(chosen)
        outs = call(
            functools.partial(
                attn_fwd_kernel, heads, ctx, rows, length, len(ins), plan if first else None, chosen
            ),
            [metas[s], *ins],
            [sds((half, 128), bf16)] * tiles
            + [sds((tiles * half, 128), f32)] * 2
            + [sds((8, 128), f32), sds((length if first else 16, 128), bf16)],
            key_scratch
            + [
                pltpu.VMEM((rows, 128), bf16),
                pltpu.VMEM((rows, 128), f32),
                pltpu.VMEM((rows, 128), f32),
                pltpu.SMEM((1,), f32),
                sems,
            ],
            2 + 9 * tiles * length / 6656,
            grid=(tiles,),
            in_specs=[smem] + [hbm] * len(ins),
            out_specs=[small] * tiles
            + [tile, tile, pl.BlockSpec((8, 128), lambda i: (0, 0)), hbm],
            deps=deps,
        )
        if first:
            kept[s] = outs[tiles + 3]
        for n, h in enumerate(chosen):
            o_mine[s][h] = outs[n]
            back[s][h] = outs[n] if h == 0 else swap(outs[n], "ctx", h * parts)
        scales[s].append((chosen, outs[tiles], outs[tiles + 1]))
        return outs[tiles + 2]

    def project(s, deps, notes):
        outs = call(
            functools.partial(proj_kernel, heads, tp),
            [place, *[back[s][h] for h in range(heads)], w_out],
            [sds((rows, every), bf16)] + [sds((own, width), bf16)] * tp,
            [pltpu.VMEM((heads, half, 128), bf16), pltpu.VMEM((rows, width), f32)],
            3,
            deps=deps,
        )
        o_nat[s] = outs[0]
        mid[s] = resid[s] + scatter_blocks(enumerate(outs[1:]), "tp", notes)

    def second_norm(s):
        normed, pull_norm2[s] = jax.vjp(layer_norm, mid[s], norm2_gain)
        normed = normed.astype(bf16)
        blocks = gather_blocks(normed)
        full2[s] = jnp.concatenate(blocks, axis=0)
        return normed, blocks[2]

    many = range(seqs)
    kept, o_nat, mid = [None] * seqs, [None] * seqs, [None] * seqs
    full2, pull_norm2 = [None] * seqs, [None] * seqs
    o_mine, back, scales = [{} for _ in many], [{} for _ in many], [[] for _ in many]
    middle = heads // 2
    plan = got[0][2]
    mark = attend(0, list(range(middle, heads)), [sents[1][0]])
    got.append(spread(1, mark[0, 0].astype(bf16)))
    grads_all = (out_grad + mark[0, 0].astype(bf16)).reshape(seqs * own, width)
    grads_all = jnp.concatenate(gather_blocks(grads_all), axis=0)
    grads_all = grads_all.reshape(tp, seqs, own, width)
    grads_all = grads_all.transpose(1, 0, 2, 3).reshape(seqs * rows, width)
    mark = attend(0, list(range(middle)), [got[1][1]])
    mark = attend(1, list(range(heads - 1, heads)), [mark])
    notes = []
    project(0, [mark], notes)
    waits = [notes[0][0]]
    for n, h in enumerate(reversed(range(heads - 1))):
        mark = attend(1, [h], [mark, *waits])
        if n == 0:
            waits = second_norm(0)
            waits, later = [waits[0]], [waits[1]]
        else:
            waits, later = later, []
    project(1, [mark], None)
    second_norm(1)

    acts, d_mid, d_pieces, gain2 = [], [], [], 0.0
    g_out_w, g_in_w, g_attn_w = 0.0, 0.0, 0.0
    for s in range(seqs):
        upper = dot(full2[s], w_in, 1, 0)
        grads = grads_all[s * rows : (s + 1) * rows]
        gated, pull_gelu = jax.vjp(
            lambda a, b: jax.nn.gelu(a, approximate=False) * b, upper[:, :ff], upper[:, ff:]
        )
        act = gated.astype(bf16)
        d_act = dot(grads, ffn_out_weight, 1, 1)
        d_upper = jnp.concatenate(pull_gelu(d_act), axis=1).astype(bf16)
        d_part = dot(d_upper, w_in, 1, 1).astype(bf16)
        d_normed2 = scatter_blocks({j: d_part[j * own : (j + 1) * own] for j in range(tp)})
        d_mid_norm, d_gain = pull_norm2[s](d_normed2)
        gain2 = gain2 + d_gain
        d_mid.append(out_grad[s].astype(f32) + d_mid_norm)
        d_pieces.append(gather_blocks(d_mid[s].astype(bf16)))
        acts.append(act)
        g_out_w = g_out_w + dot(act, grads, 0, 0)
        g_in_w = g_in_w + dot(full2[s], d_upper, 0, 0)
    ready = [g_in_w.astype(bf16), g_out_w.astype(bf16)]
    early = lax.psum(ready, "ctx")

    d_all, in_grad, gain1 = [], [], 0.0
    backward_cost = [1, 1]
    for s in range(seqs):
        outs = call(
            functools.partial(d_attn_kernel, heads, tp),
            [place, *d_pieces[s], w_out],
            [sds((rows, width), bf16)] + [sds((half, 128), bf16)] * heads,
            [pltpu.VMEM((rows, width), f32), pltpu.VMEM((heads, half, 128), bf16)],
            4,
            deps=ready if s else [],
        )
        g_attn_w = g_attn_w + dot(o_nat[s], outs[0], 0, 0)
        d = outs[1:]
        d_attn = [d[0]] + [swap(d[h], "ctx", h * parts) for h in range(1, heads)]
        if s == seqs - 1:
            g_attn_w = lax.psum(g_attn_w, "ctx")
        outs = call(
            functools.partial(
                attn_bwd_kernel, heads, ctx, rows, length, [g[0] for g in scales[s]]
            ),
            [
                metas[s],
                *d_attn,
                *[o_mine[s][h] for h in range(heads)],
                *[g[1] for g in scales[s]],
                *[g[2] for g in scales[s]],
                *mines[s],
                kept[s],
            ],
            [sds((half, 128), bf16)] * heads
            + [sds((heads * rows, 128), bf16)] * parts
            + [sds((16, 128), bf16)],
            key_scratch
            + [
                pltpu.VMEM((heads, half, 128), bf16),
                pltpu.VMEM((heads, half, 128), bf16),
                pltpu.VMEM((heads * half, 128), f32),
                pltpu.VMEM((heads * half, 128), f32),
                pltpu.VMEM((rows, 128), bf16),
                pltpu.VMEM((rows, 128), bf16),
                pltpu.VMEM((64, rows), bf16),
                pltpu.VMEM((64, rows), bf16),
                pltpu.VMEM((rows, 128), f32),
                pltpu.VMEM((128, length), f32),
                pltpu.VMEM((length, 128), bf16),
                sems,
            ],
            backward_cost[s],
            grid=(heads,),
            in_specs=[smem]
            + [small] * (2 * heads)
            + [pl.BlockSpec((len(g[0]) * half, 128), lambda i: (0, 0)) for g in scales[s]] * 2
            + [hbm] * (heads + 1),
            out_specs=[small] * heads
            + [hbm] * parts
            + [pl.BlockSpec((16, 128), lambda i: (0, 0))],
            deps=ready,
        )
        ready = [outs[0]]
        if s == 0:
            act = jnp.concatenate(acts, axis=0) + outs[-1][0, 0]
        dkv = scatter_blocks(enumerate(outs[heads:-1]), "ctx")
        sent = [
            jnp.concatenate([dkv[h * rows : (h + 1) * rows].astype(bf16), outs[h]], axis=0)
            for h in range(heads)
        ]
        back = [sent[0]] + [swap(sent[h], "ctx", h * parts) for h in range(1, heads)]
        outs = call(
            functools.partial(d_qkv_kernel, heads, tp, half),
            [place, *back, w_all, *tables, full1[s]],
            [sds((rows, 3 * every), bf16), sds((1, width), f32)]
            + [sds((own, width), bf16)] * tp,
            [pltpu.VMEM((heads, rows + half, 128), bf16), pltpu.VMEM((rows, width), f32)],
            6,
        )
        d_all.append(outs[0])
        gain1 = gain1 + outs[1][0]
        _, pull_norm1 = jax.vjp(lambda r: layer_norm(r, norm1_gain), resid[s])
        d_in_norm = pull_norm1(scatter_blocks(enumerate(outs[2:])))[0]
        in_grad.append((d_mid[s] + d_in_norm).astype(bf16))
    g_qkv_w = sum(dot(full1[s], d_all[s], 0, 0) for s in range(seqs))
    orders = [row_order(ctx, turn) for turn in range(2)]
    dealt = call(
        functools.partial(deal_kernel, [o[1] for o in orders]),
        [place, g_qkv_w],
        [sds((width // 2, 3 * every // 2), bf16)] * 4,
        [],
        3,
        deps=early,
    )
    sums = []
    for turn in range(2):
        sums += sum_halves(dealt[2 * turn], dealt[2 * turn + 1], "ctx", orders[turn][0])
    (g_qkv_w,) = call(
        functools.partial(undeal_kernel, [o[1] for o in orders], 4),
        [place, *sums],
        [sds((width, 3 * every), f32)],
        [],
        3,
    )
    g_qkv_w = g_qkv_w.reshape(width, 3, heads, head_dim)

    out_part = dot(act, ffn_out_weight, 1, 0).astype(bf16).reshape(seqs, tp, own, width)
    ffn_sum = scatter_blocks({j: out_part[:, j] for j in range(tp)})
    block_out = (jnp.stack(mid) + ffn_sum).astype(bf16)

    gains = total(total(jnp.stack([gain1 / norm1_gain, gain2]), "tp"), "ctx")
    return (
        block_out,
        jnp.stack(in_grad),
        gains[0],
        g_qkv_w,
        g_attn_w.reshape(heads, head_dim, width),
        gains[1],
        early[0].astype(f32).reshape(width, 2, ff),
        early[1].astype(f32),
    )


def solution(mesh):
    in_specs = (
        P(None, ("ctx", "tp"), None),
        P(),
        P(None, None, "tp", None),
        P("tp", None, None),
        P(),
        P(None, None, "tp"),
        P("tp", None),
        P(None, "ctx"),
        P(None, ("ctx", "tp"), None),
    )
    out_specs = (
        P(None, ("ctx", "tp"), None),
        P(None, ("ctx", "tp"), None),
        P(),
        P(None, None, "tp", None),
        P("tp", None, None),
        P(),
        P(None, None, "tp"),
        P("tp", None),
    )
    return jax.shard_map(shards, mesh=mesh, in_specs=in_specs, out_specs=out_specs, check_vma=False)
```

```python
import functools
import math

import jax
import jax.numpy as jnp
from jax import lax
from jax.experimental import pallas as pl
from jax.experimental.pallas import tpu as pltpu
from jax.sharding import PartitionSpec as P

theta_log = math.log(160000.0)
neg_fill = -1e30
safe_bound = 60.0
log2_e = math.log2(math.e)
wide_keys = 1664
fine_keys = 512
cut_count = 4
bf16 = jnp.bfloat16
f32 = jnp.float32
vmem_limit = 56 * 2**20


def swap(block, axis, bits):
    size = lax.axis_size(axis)
    return lax.ppermute(block, axis, [(i, i ^ bits) for i in range(size)])


def bit_list(size):
    bits, b = [], 1
    while b < size:
        bits.append(b)
        b *= 2
    return bits


def total(value, axis):
    for b in bit_list(lax.axis_size(axis)):
        value = value + swap(value, axis, b)
    return value


def gate(array):
    return jnp.minimum(jnp.abs(array[(0,) * array.ndim]), 0)


def gather_blocks(block, axis="tp", bits=None):
    held = {0: block}
    for b in reversed(bit_list(lax.axis_size(axis)) if bits is None else bits):
        for j in list(held):
            held[j ^ b] = swap(held[j], axis, b)
    return [held[j] for j in sorted(held)]


def scatter_blocks(blocks, axis="tp", notes=None):
    held = dict(blocks)
    for b in bit_list(max(held) + 1):
        for j in sorted(held):
            if j & b:
                got = swap(held.pop(j), axis, b)
                summed = held[j ^ b].astype(f32) + got.astype(f32)
                held[j ^ b] = summed if len(held) == 1 else summed.astype(bf16)
        if notes is not None:
            notes.append(list(held.values()))
    return held[0]


def row_order(size, turn):
    bits = bit_list(size)
    bits = bits[turn:] + bits[:turn]
    return bits, sorted(range(size), key=lambda k: [k & b for b in bits])


def sum_halves(keep, send, axis, bits):
    for n, b in enumerate(bits):
        held = (keep.astype(f32) + swap(send, axis, b).astype(f32)).astype(bf16)
        if n < len(bits) - 1:
            mid = held.shape[0] // 2
            keep, send = held[:mid], held[mid:]
    for b in reversed(bits[1:]):
        held = jnp.concatenate([held, swap(held, axis, b)], axis=0)
    return held, swap(held, axis, bits[0])


def dot(a, b, ca, cb):
    return lax.dot_general(a, b, (((ca,), (cb,)), ((), ())), preferred_element_type=f32)


def lanes():
    return lax.broadcasted_iota(jnp.int32, (1, 128), 1)


def rot(u):
    first = (lanes() & 63) < 32
    return jnp.where(first, -pltpu.roll(u, 96, 1), pltpu.roll(u, 32, 1))


def rot_back(w):
    first = (lanes() & 63) < 32
    return jnp.where(first, pltpu.roll(w, 96, 1), -pltpu.roll(w, 32, 1))


def call(
    kernel,
    ins,
    outs,
    scratch,
    cost,
    smem_ins=1,
    grid=None,
    in_specs=None,
    out_specs=None,
    deps=(),
):
    whole = pl.BlockSpec(memory_space=pltpu.VMEM)
    if in_specs is None:
        in_specs = [pl.BlockSpec(memory_space=pltpu.SMEM)] * smem_ins + [whole] * (
            len(ins) - smem_ins
        )
        out_specs = [whole] * len(outs)
    extra = {} if grid is None else {"grid": grid}
    moved = sum(a.size * a.dtype.itemsize for a in [*ins, *outs])
    time = int(cost * 1.15e9)
    used = len(ins)
    ins = [*ins, *deps]
    in_specs = in_specs + [pl.BlockSpec(memory_space=pl.ANY)] * len(deps)

    def body(*refs):
        kernel(*refs[:used], *refs[len(ins) :])

    return pl.pallas_call(
        body,
        in_specs=in_specs,
        out_specs=out_specs,
        out_shape=outs,
        scratch_shapes=scratch,
        compiler_params=pltpu.CompilerParams(vmem_limit_bytes=vmem_limit),
        cost_estimate=pl.CostEstimate(
            flops=time, transcendentals=0, bytes_accessed=int(moved)
        ),
        **extra,
    )(*ins)


def assemble(meta, pieces, x_scr):
    part = pieces[0].shape[0]
    for j, piece in enumerate(pieces):
        at = pl.multiple_of((meta[2] ^ j) * part, 8)
        x_scr[pl.ds(at, part), :] = piece[...].astype(f32)


def disperse(meta, x_scr, pieces):
    part = pieces[0].shape[0]
    for j, piece in enumerate(pieces):
        at = pl.multiple_of((meta[2] ^ j) * part, 8)
        piece[...] = x_scr[pl.ds(at, part), :].astype(bf16)


def pair(u, v):
    return jnp.where(lanes() < 64, u, pltpu.roll(v, 64, 1))


def pair_right(u, v):
    return jnp.where(lanes() < 64, pltpu.roll(u, 64, 1), v)


def qkv_kernel(heads, tp, half, scale, meta, *refs):
    pieces, refs = refs[:tp], refs[tp:]
    weight, cosine, sine, x_ref, zero, *refs = refs
    zero[...] = jnp.zeros_like(zero)
    outs, (x_scr, kv_scr, q_scr) = refs[:heads], refs[heads:]
    assemble(meta, pieces, x_scr)
    x = x_scr[...].astype(bf16)
    x_ref[...] = x
    every = heads * 64
    for t in range(heads // 2):
        q, k, v = [
            dot(x, weight[:, n * every + t * 128 : n * every + (t + 1) * 128], 1, 0)
            for n in range(3)
        ]
        q = (q * cosine[...] + rot(q) * sine[...]) * scale
        k = k * cosine[...] + rot(k) * sine[...]
        kv_scr[2 * t] = pair(k, v).astype(bf16)
        kv_scr[2 * t + 1] = pair_right(k, v).astype(bf16)
        q_scr[2 * t] = pair(q[:half], q[half:]).astype(bf16)
        q_scr[2 * t + 1] = pair_right(q[:half], q[half:]).astype(bf16)
    for kh in range(heads):
        outs[kh][: 2 * half, :] = kv_scr[meta[1] ^ kh]
        outs[kh][2 * half :, :] = q_scr[meta[1] ^ kh]


def row_range(tok, meta, length):
    low = jnp.zeros_like(tok)
    high = jnp.full_like(tok, length)
    for d in range(cut_count):
        c = meta[3 + d]
        low = jnp.where(tok >= c, jnp.maximum(low, c), low)
        high = jnp.where(tok < c, jnp.minimum(high, c), high)
    return low, high


def load_keys(meta, rows, plan, got, kvs, vx, q_scr, sems):
    heads = q_scr.shape[0]
    copies = []
    for c in range(heads):
        source = got[c].at[pl.ds(rows, rows // 2)]
        copies.append(pltpu.make_async_copy(source, q_scr.at[c], sems.at[c]))
    if plan is None:
        copies.append(pltpu.make_async_copy(got[heads], kvs, sems.at[heads]))
    else:
        for n, (ref, start, k) in enumerate(plan):
            at = pl.multiple_of((meta[0] ^ k) * rows, rows)
            source = got[ref].at[pl.ds(start, rows)]
            target = kvs.at[pl.ds(at, rows)]
            copies.append(pltpu.make_async_copy(source, target, sems.at[heads + n]))
    for c in copies:
        c.start()
    for c in copies:
        c.wait()
    vx[...] = jnp.where(lanes() < 64, jnp.ones((), bf16), kvs[...])


def attn_fwd_kernel(heads, ctx, rows, length, count, plan, chosen, meta, *refs):
    got, refs = refs[:count], refs[count:]
    o_refs, refs = refs[: len(chosen)], refs[len(chosen) :]
    linv_ref, m_ref, zero, kv_out, kvs, vx, q_scr, qc, acc, m_scr, norms, sems = refs
    half = rows // 2
    turn = pl.program_id(0)
    i = turn + chosen[0]
    left = lanes() < 64

    @pl.when(turn == 0)
    def _():
        zero[...] = jnp.zeros_like(zero)
        load_keys(meta, rows, plan, got, kvs, vx, q_scr, sems)
        if plan is not None:
            keep = pltpu.make_async_copy(kvs, kv_out, sems.at[0])
            keep.start()
        k = jnp.where(left, kvs[...].astype(f32), 0.0)
        norms[0] = jnp.max(jnp.sum(k * k, axis=1, keepdims=True))
        if plan is not None:
            keep.wait()

    q = q_scr[i].astype(f32)
    qa = jnp.where(left, q, 0.0)
    qb = jnp.where(left, pltpu.roll(q, 64, 1), 0.0)
    qc[:half] = qa.astype(bf16)
    qc[half:] = qb.astype(bf16)
    q_norm = jnp.max(jnp.sum(jnp.maximum(qa * qa, qb * qb), axis=1, keepdims=True))
    safe = q_norm * norms[0] < safe_bound * safe_bound
    single = meta[3] >= length
    fast = jnp.logical_and(safe, single)
    acc[...] = jnp.zeros_like(acc)
    m_scr[...] = jnp.zeros_like(m_scr)

    @pl.when(fast)
    def _():
        def step(j, _):
            keys = pl.ds(pl.multiple_of(j * wide_keys, wide_keys), wide_keys)
            e = jnp.exp2(dot(qc[...], kvs[keys, :], 1, 1)).astype(bf16)
            acc[...] += dot(e, vx[keys, :], 1, 0)
            return 0

        lax.fori_loop(0, length // wide_keys, step, 0)

    @pl.when(jnp.logical_not(fast))
    def _():
        first = (meta[0] ^ (i * (ctx // heads))) * rows
        tok = first + lax.broadcasted_iota(jnp.int32, (rows, 1), 0)
        low, high = row_range(tok, meta, length)
        j_low = lax.div(row_range(first, meta, length)[0], fine_keys)
        j_high = lax.div(row_range(first + rows - 1, meta, length)[1] + fine_keys - 1, fine_keys)

        def masked(j):
            keys = pl.ds(pl.multiple_of(j * fine_keys, fine_keys), fine_keys)
            spot = j * fine_keys + lax.broadcasted_iota(jnp.int32, (1, fine_keys), 1)
            allowed = jnp.logical_and(spot >= low, spot < high)
            return keys, allowed, dot(qc[...], kvs[keys, :], 1, 1)

        @pl.when(jnp.logical_not(safe))
        def _():
            m_scr[...] = jnp.full_like(m_scr, neg_fill)

            def peak(j, _):
                _, allowed, s = masked(j)
                s = jnp.max(jnp.where(allowed, s, neg_fill), axis=1, keepdims=True)
                m_scr[...] = jnp.maximum(m_scr[...], s)
                return 0

            lax.fori_loop(j_low, j_high, peak, 0)

        def step(j, _):
            keys, allowed, s = masked(j)
            e = jnp.where(allowed, jnp.exp2(s - m_scr[:, 0:1]), 0.0).astype(bf16)
            acc[...] += dot(e, vx[keys, :], 1, 0)
            return 0

        lax.fori_loop(j_low, j_high, step, 0)

    a = acc[...]
    o = a / pltpu.roll(a, 64, 1)
    out = jnp.where(left, pltpu.roll(o[:half], 64, 1), o[half:]).astype(bf16)
    for c in range(len(chosen)):

        @pl.when(turn == c)
        def _(c=c):
            o_refs[c][...] = out

    inv = 1.0 / a
    linv_ref[...] = jnp.where(left, inv[:half], pltpu.roll(inv[half:], 64, 1))
    m_ref[...] = jnp.where(left, m_scr[:half], m_scr[half:])


def attn_bwd_kernel(heads, ctx, rows, length, groups, meta, *refs):
    do_refs, refs = refs[:heads], refs[heads:]
    o_refs, refs = refs[:heads], refs[heads:]
    linv_refs, refs = refs[: len(groups)], refs[len(groups) :]
    m_refs, refs = refs[: len(groups)], refs[len(groups) :]
    got, refs = refs[: heads + 1], refs[heads + 1 :]
    dq_refs, refs = refs[:heads], refs[heads:]
    parts = ctx // heads
    dkv_refs, zero, refs = refs[:parts], refs[parts], refs[parts + 1 :]
    kvs, vx, q_scr, do_scr, o_scr, linv_scr, m_scr, *refs = refs
    qc, dc, qt, dt, dq_acc, dkv_t, dkv_n, sems = refs
    half = rows // 2
    i = pl.program_id(0)
    lane = lanes()
    left = lane < 64

    @pl.when(i == 0)
    def _():
        load_keys(meta, rows, None, got, kvs, vx, q_scr, sems)
        zero[...] = jnp.zeros_like(zero)
        dkv_t[...] = jnp.zeros_like(dkv_t)
        for c in range(heads):
            do_scr[c] = do_refs[c][...]
            o_scr[c] = o_refs[c][...]
        for n, g in enumerate(groups):
            side = slice(g[0] * half, (g[-1] + 1) * half)
            linv_scr[side, :] = linv_refs[n][...]
            m_scr[side, :] = m_refs[n][...]

    q = q_scr[i].astype(f32)
    here = pl.ds(pl.multiple_of(i * half, half), half)
    do = do_scr[i].astype(f32) * linv_scr[here, :]
    prod = do * o_scr[i].astype(f32)
    delta_a = jnp.sum(jnp.where(left, prod, 0.0), axis=1, keepdims=True)
    delta_b = jnp.sum(jnp.where(left, 0.0, prod), axis=1, keepdims=True)

    def extended(x, delta):
        coarse = delta.astype(bf16).astype(f32)
        ends = jnp.where(lane == 0, -coarse, jnp.where(lane == 1, coarse - delta, 0.0))
        return jnp.where(left, ends, x).astype(bf16)

    qc[:half] = jnp.where(left, q, 0.0).astype(bf16)
    qc[half:] = jnp.where(left, pltpu.roll(q, 64, 1), 0.0).astype(bf16)
    dc[:half] = extended(pltpu.roll(do, 64, 1), delta_a)
    dc[half:] = extended(do, delta_b)
    qt[...] = qc[...].astype(f32).T[:64].astype(bf16)
    dt[...] = dc[...].astype(f32).T[64:].astype(bf16)
    dq_acc[...] = jnp.zeros_like(dq_acc)
    shift = m_scr[here, :]
    shifted = jnp.max(jnp.abs(shift)) > 0.0
    single = meta[3] >= length
    fast = jnp.logical_and(single, jnp.logical_not(shifted))

    def accumulate(keys, e, allowed):
        ds = e * dot(dc[...], vx[keys, :], 1, 1)
        if allowed is not None:
            ds = jnp.where(allowed, ds, 0.0)
        ds = ds.astype(bf16)
        e = e.astype(bf16)
        dq_acc[...] += dot(ds, kvs[keys, :], 1, 0)
        dkv_t[:64, keys] += dot(qt[...], ds, 1, 0)
        dkv_t[64:, keys] += dot(dt[...], e, 1, 0)

    @pl.when(fast)
    def _():
        def step(j, _):
            keys = pl.ds(pl.multiple_of(j * wide_keys, wide_keys), wide_keys)
            accumulate(keys, jnp.exp2(dot(qc[...], kvs[keys, :], 1, 1)), None)
            return 0

        lax.fori_loop(0, length // wide_keys, step, 0)

    @pl.when(jnp.logical_not(fast))
    def _():
        first = (meta[0] ^ (i * (ctx // heads))) * rows
        tok = first + lax.broadcasted_iota(jnp.int32, (rows, 1), 0)
        low, high = row_range(tok, meta, length)
        j_low = lax.div(row_range(first, meta, length)[0], fine_keys)
        j_high = lax.div(row_range(first + rows - 1, meta, length)[1] + fine_keys - 1, fine_keys)
        m = jnp.concatenate([shift[:, 0:1], shift[:, 64:65]], axis=0)

        def step(j, _):
            keys = pl.ds(pl.multiple_of(j * fine_keys, fine_keys), fine_keys)
            spot = j * fine_keys + lax.broadcasted_iota(jnp.int32, (1, fine_keys), 1)
            allowed = jnp.logical_and(spot >= low, spot < high)
            s = dot(qc[...], kvs[keys, :], 1, 1)
            e = jnp.where(allowed, jnp.exp2(s - m), 0.0)
            accumulate(keys, e, allowed)
            return 0

        lax.fori_loop(j_low, j_high, step, 0)

    a = dq_acc[...] * 0.125
    out = jnp.where(left, a[:half], pltpu.roll(a[half:], 64, 1)).astype(bf16)
    for c in range(heads):

        @pl.when(i == c)
        def _(c=c):
            dq_refs[c][...] = out

    @pl.when(i == heads - 1)
    def _():
        is_key = lax.broadcasted_iota(jnp.int32, (128, 1), 0) < 64
        for j in range(length // wide_keys):
            part = dkv_t[:, j * wide_keys : (j + 1) * wide_keys]
            part = jnp.where(is_key, part * math.log(2.0), part)
            dkv_n[j * wide_keys : (j + 1) * wide_keys, :] = part.T.astype(bf16)
        copies = []
        for k in range(ctx):
            at = pl.multiple_of((meta[0] ^ k) * rows, rows)
            target = dkv_refs[k % parts].at[pl.ds(k // parts * rows, rows)]
            copies.append(pltpu.make_async_copy(dkv_n.at[pl.ds(at, rows)], target, sems.at[k]))
        for c in copies:
            c.start()
        for c in copies:
            c.wait()


def proj_kernel(heads, tp, meta, *refs):
    o_refs, refs = refs[:heads], refs[heads:]
    weight, o_nat, *refs = refs
    pieces, (o_scr, x_scr) = refs[:tp], refs[tp:]
    half = o_refs[0].shape[0]
    for kh in range(heads):
        o_scr[meta[1] ^ kh] = o_refs[kh][...]
    for t in range(heads // 2):
        u, v = o_scr[2 * t].astype(f32), o_scr[2 * t + 1].astype(f32)
        o_nat[:half, t * 128 : (t + 1) * 128] = pair(u, v).astype(bf16)
        o_nat[half:, t * 128 : (t + 1) * 128] = pair_right(u, v).astype(bf16)
    x_scr[...] = dot(o_nat[...], weight[...], 1, 0)
    disperse(meta, x_scr, pieces)


def d_attn_kernel(heads, tp, meta, *refs):
    pieces, refs = refs[:tp], refs[tp:]
    weight, full, zero, *refs = refs
    zero[...] = jnp.zeros_like(zero)
    outs, (x_scr, d_scr) = refs[:heads], refs[heads:]
    half = outs[0].shape[0]
    assemble(meta, pieces, x_scr)
    x = x_scr[...].astype(bf16)
    full[...] = x
    for t in range(heads // 2):
        d = dot(x, weight[t * 128 : (t + 1) * 128, :], 1, 1)
        d_scr[2 * t] = pair(d[:half], d[half:]).astype(bf16)
        d_scr[2 * t + 1] = pair_right(d[:half], d[half:]).astype(bf16)
    for kh in range(heads):
        outs[kh][...] = d_scr[meta[1] ^ kh]


def d_qkv_kernel(heads, tp, half, meta, *refs):
    got, refs = refs[:heads], refs[heads:]
    weight, cosine, sine, normed, d_all, gain, *refs = refs
    pieces, (scr, x_scr) = refs[:tp], refs[tp:]
    every = heads * 64
    for kh in range(heads):
        scr[meta[1] ^ kh] = got[kh][...]
    for t in range(heads // 2):
        u, v = scr[2 * t].astype(f32), scr[2 * t + 1].astype(f32)
        dk, dv = pair(u[: 2 * half], v[: 2 * half]), pair_right(u[: 2 * half], v[: 2 * half])
        u, v = u[2 * half :], v[2 * half :]
        dq = jnp.concatenate([pair(u, v), pair_right(u, v)], axis=0)
        dq = dq * cosine[...] + rot_back(dq * sine[...])
        dk = dk * cosine[...] + rot_back(dk * sine[...])
        for n, d in enumerate((dq, dk, dv)):
            d_all[:, n * every + t * 128 : n * every + (t + 1) * 128] = d.astype(bf16)
    x_scr[...] = dot(d_all[...], weight[...], 1, 1)
    gain[...] = jnp.sum(x_scr[...] * normed[...].astype(f32), axis=0, keepdims=True)
    disperse(meta, x_scr, pieces)


def deal_kernel(orders, meta, grad, other, *outs):
    part, wide = grad.shape[0] // len(orders[0]), outs[0].shape[1]
    split = grad.shape[1] - wide
    deep = len(orders[0]) // 2
    for c, order in enumerate(orders):
        for n, k in enumerate(order):
            at = pl.ds(pl.multiple_of((meta[0] ^ k) * part, part), part)
            out, place = outs[2 * c + n // deep], pl.ds(n % deep * part, part)
            if c == 0:
                out[place, :] = grad[at, :wide].astype(bf16)
            else:
                out[place, :split] = grad[at, wide:].astype(bf16)
                out[place, split:] = other[at, :].astype(bf16)


def undeal_kernel(orders, meta, *refs):
    ins, (grad, other) = refs[:4], refs[4:]
    part, wide = grad.shape[0] // len(orders[0]), ins[0].shape[1]
    split = grad.shape[1] - wide
    deep = len(orders[0]) // 2
    for c, order in enumerate(orders):
        for n, k in enumerate(order):
            at = pl.ds(pl.multiple_of((meta[0] ^ k) * part, part), part)
            block = ins[2 * c + n // deep][n % deep * part : (n % deep + 1) * part, :].astype(f32)
            if c == 0:
                grad[at, :wide] = block
            else:
                grad[at, wide:] = block[:, :split]
                other[at, :] = block[:, split:]


def rope_tables(positions, width):
    freqs = jnp.exp(-(2.0 * jnp.arange(width // 2, dtype=f32) / width) * theta_log)
    angles = positions.astype(f32)[:, None] * freqs[None, :]
    cosine, sine = jnp.cos(angles), jnp.sin(angles)
    lay = lambda u: jnp.concatenate([u, u, u, u], axis=1)
    return lay(cosine), lay(sine)


def layer_norm(rows, gain):
    mean = jnp.mean(rows, axis=-1, keepdims=True)
    cent = rows - mean
    var = jnp.mean(cent * cent, axis=-1, keepdims=True)
    return cent * lax.rsqrt(var + 1e-05) * gain


def shards(
    hidden_in,
    norm1_gain,
    qkv_weight,
    attn_weight,
    norm2_gain,
    ffn_in_weight,
    ffn_out_weight,
    doc_ids,
    out_grad,
):
    seqs = hidden_in.shape[0]
    width = hidden_in.shape[2]
    heads = qkv_weight.shape[2]
    head_dim = qkv_weight.shape[3]
    rows = doc_ids.shape[1]
    half = rows // 2
    ff = ffn_out_weight.shape[0]
    ctx, tp = lax.axis_size("ctx"), lax.axis_size("tp")
    parts = ctx // heads
    length = ctx * rows
    own = rows // tp
    me, spot = lax.axis_index("ctx"), lax.axis_index("tp")
    sds = jax.ShapeDtypeStruct

    steps = jnp.arange(1, cut_count + 1, dtype=jnp.int32)
    counts = jnp.sum((doc_ids[:, :, None] < steps).astype(f32), axis=1)
    cuts = total(counts, "ctx").astype(jnp.int32)
    place = jnp.stack([me, me // parts, spot]).astype(jnp.int32)
    metas = [jnp.concatenate([place, cuts[s]]) for s in range(seqs)]

    every = heads * head_dim
    w_all = qkv_weight.reshape(width, 3 * every)
    w_out = attn_weight.reshape(every, width)
    w_in = ffn_in_weight.reshape(width, 2 * ff)
    tables = rope_tables(me * rows + jnp.arange(rows, dtype=jnp.int32), head_dim)
    scale = log2_e / math.sqrt(head_dim)

    resid = [hidden_in[s].astype(f32) for s in range(seqs)]
    full1, sents, mines = [], [], []

    def spread(s, zero):
        mine = mines[s]
        rest = jnp.concatenate([m[:rows] for m in mine], axis=0) + zero
        held = [(rest, [h * parts for h in range(heads)])]
        plan = [(h, 0, h * parts) for h in range(heads)]
        arrays = list(mine)
        for b in bit_list(parts):
            for block, ks in list(held):
                ks = [k ^ b for k in ks]
                held.append((swap(block, "ctx", b), ks))
                plan += [(len(arrays), n * rows, k) for n, k in enumerate(ks)]
                arrays.append(held[-1][0])
        return arrays, rest, plan

    for s in range(seqs):
        blocks = gather_blocks(layer_norm(resid[s], norm1_gain).astype(bf16))
        outs = call(
            functools.partial(qkv_kernel, heads, tp, half, scale),
            [place, *blocks, w_all, *tables],
            [sds((rows, width), bf16), sds((16, 128), bf16)]
            + [sds((rows + half, 128), bf16)] * heads,
            [
                pltpu.VMEM((rows, width), f32),
                pltpu.VMEM((heads, rows, 128), bf16),
                pltpu.VMEM((heads, half, 128), bf16),
            ],
            7,
            deps=[got[0][1], cuts] if s else [],
        )
        full1.append(outs[0])
        sent = outs[2:]
        sents.append(sent)
        sent_zero = outs[1][0, 0]
        mines.append([sent[0]] + [swap(sent[h], "ctx", h * parts) for h in range(1, heads)])
        if s == 0:
            got = [spread(0, jnp.zeros((), bf16))]

    smem = pl.BlockSpec(memory_space=pltpu.SMEM)
    hbm = pl.BlockSpec(memory_space=pl.ANY)
    small = pl.BlockSpec((half, 128), lambda i: (0, 0))
    tile = pl.BlockSpec((half, 128), lambda i: (i, 0))
    key_scratch = [
        pltpu.VMEM((length, 128), bf16),
        pltpu.VMEM((length, 128), bf16),
        pltpu.VMEM((heads, half, 128), bf16),
    ]
    sems = pltpu.SemaphoreType.DMA((ctx + heads,))

    def attend(s, chosen, deps):
        first = kept[s] is None
        ins = got[s][0] if first else [*mines[s], kept[s]]
        tiles = len(chosen)
        outs = call(
            functools.partial(
                attn_fwd_kernel, heads, ctx, rows, length, len(ins), plan if first else None, chosen
            ),
            [metas[s], *ins],
            [sds((half, 128), bf16)] * tiles
            + [sds((tiles * half, 128), f32)] * 2
            + [sds((8, 128), f32), sds((length if first else 16, 128), bf16)],
            key_scratch
            + [
                pltpu.VMEM((rows, 128), bf16),
                pltpu.VMEM((rows, 128), f32),
                pltpu.VMEM((rows, 128), f32),
                pltpu.SMEM((1,), f32),
                sems,
            ],
            2 + 9 * tiles * length / 6656,
            grid=(tiles,),
            in_specs=[smem] + [hbm] * len(ins),
            out_specs=[small] * tiles
            + [tile, tile, pl.BlockSpec((8, 128), lambda i: (0, 0)), hbm],
            deps=deps,
        )
        if first:
            kept[s] = outs[tiles + 3]
        for n, h in enumerate(chosen):
            o_mine[s][h] = outs[n]
            back[s][h] = outs[n] if h == 0 else swap(outs[n], "ctx", h * parts)
        scales[s].append((chosen, outs[tiles], outs[tiles + 1]))
        return outs[tiles + 2]

    def project(s, deps, notes):
        outs = call(
            functools.partial(proj_kernel, heads, tp),
            [place, *[back[s][h] for h in range(heads)], w_out],
            [sds((rows, every), bf16)] + [sds((own, width), bf16)] * tp,
            [pltpu.VMEM((heads, half, 128), bf16), pltpu.VMEM((rows, width), f32)],
            3,
            deps=deps,
        )
        o_nat[s] = outs[0]
        mid[s] = resid[s] + scatter_blocks(enumerate(outs[1:]), "tp", notes)

    def second_norm(s, zero):
        normed, pull_norm2[s] = jax.vjp(layer_norm, mid[s] + zero, norm2_gain)
        normed = normed.astype(bf16)
        blocks = gather_blocks(normed)
        full2[s] = jnp.concatenate(blocks, axis=0)
        return normed, blocks[2]

    many = range(seqs)
    kept, o_nat, mid = [None] * seqs, [None] * seqs, [None] * seqs
    full2, pull_norm2 = [None] * seqs, [None] * seqs
    o_mine, back, scales = [{} for _ in many], [{} for _ in many], [[] for _ in many]
    plan = got[0][2]
    grads_all = (out_grad + sent_zero).reshape(seqs * own, width)
    grad_blocks = gather_blocks(grads_all)
    grads_all = jnp.concatenate(grad_blocks, axis=0).reshape(tp, seqs, own, width)
    grads_all = grads_all.transpose(1, 0, 2, 3).reshape(seqs * rows, width)
    got.append(spread(1, jnp.zeros((), bf16)))
    mark = attend(0, list(range(heads)), [got[1][1], grad_blocks[2]])
    mark = attend(1, list(range(heads - 1, heads)), [mark])
    notes = []
    project(0, [mark], notes)
    waits = [notes[0][0]]
    for n, h in enumerate(reversed(range(heads - 1))):
        mark = attend(1, [h], [mark, *waits])
        if n == 0:
            waits = second_norm(0, mark[0, 0])
            waits, later = [waits[0]], [waits[1]]
        else:
            waits, later = later, []
    notes = []
    project(1, [mark], notes)
    full2[0] = full2[0] + gate(notes[0][0])
    second_norm(1, 0.0)

    acts, d_mid, d_pieces, gain2 = [], [], [], 0.0

    def to_heads(s, deps):
        outs = call(
            functools.partial(d_attn_kernel, heads, tp),
            [place, *d_pieces[s], w_out],
            [sds((rows, width), bf16), sds((16, 128), bf16)] + [sds((half, 128), bf16)] * heads,
            [pltpu.VMEM((rows, width), f32), pltpu.VMEM((heads, half, 128), bf16)],
            4,
            deps=deps,
        )
        d = outs[2:]
        d = [d[0]] + [swap(d[h], "ctx", h * parts) for h in range(1, heads)]
        return outs[0], d, outs[1][0, 0]

    zero = jnp.zeros((), bf16)
    g_out_w, g_in_w = 0.0, 0.0
    for s in range(seqs):
        upper = dot(full2[s], w_in, 1, 0)
        grads = grads_all[s * rows : (s + 1) * rows]
        gated, pull_gelu = jax.vjp(
            lambda a, b: jax.nn.gelu(a, approximate=False) * b, upper[:, :ff], upper[:, ff:]
        )
        act = gated.astype(bf16)
        d_act = dot(grads, ffn_out_weight, 1, 1)
        d_upper = jnp.concatenate(pull_gelu(d_act), axis=1).astype(bf16)
        d_part = dot(d_upper + zero, w_in, 1, 1).astype(bf16)
        notes = []
        d_normed2 = scatter_blocks(
            {j: d_part[j * own : (j + 1) * own] for j in range(tp)}, "tp", notes
        )
        d_mid_norm, d_gain = pull_norm2[s](d_normed2)
        gain2 = gain2 + d_gain
        d_mid.append(out_grad[s].astype(f32) + d_mid_norm)
        d_pieces.append(gather_blocks(d_mid[s].astype(bf16)))
        if s == 0:
            dmid_full, d_attn, zero = to_heads(0, [])
            g_attn_w = dot(dmid_full, o_nat[0], 0, 0)
        acts.append(act)
        g_out_w = g_out_w + dot(act, grads, 0, 0)
        g_in_w = g_in_w + dot(d_upper, full2[s], 0, 0)
    g_in_w = g_in_w + gate(d_attn[heads - 1]).astype(f32)
    ready = [g_in_w.astype(bf16), g_out_w.astype(bf16)]
    early = lax.psum(ready, "ctx")
    ready = [g[:16, :128] for g in ready] + notes[0][:1]

    in_grad, gain1, zeros, d_got = [], 0.0, [], []
    backward_cost = [1, 1]
    for s in range(seqs):
        if s == seqs - 1:
            dmid_full, d_attn, _ = to_heads(s, ready)
            g_attn_w = g_attn_w + dot(dmid_full, o_nat[s], 0, 0)
        outs = call(
            functools.partial(
                attn_bwd_kernel, heads, ctx, rows, length, [g[0] for g in scales[s]]
            ),
            [
                metas[s],
                *d_attn,
                *[o_mine[s][h] for h in range(heads)],
                *[g[1] for g in scales[s]],
                *[g[2] for g in scales[s]],
                *mines[s],
                kept[s],
            ],
            [sds((half, 128), bf16)] * heads
            + [sds((heads * rows, 128), bf16)] * parts
            + [sds((16, 128), bf16)],
            key_scratch
            + [
                pltpu.VMEM((heads, half, 128), bf16),
                pltpu.VMEM((heads, half, 128), bf16),
                pltpu.VMEM((heads * half, 128), f32),
                pltpu.VMEM((heads * half, 128), f32),
                pltpu.VMEM((rows, 128), bf16),
                pltpu.VMEM((rows, 128), bf16),
                pltpu.VMEM((64, rows), bf16),
                pltpu.VMEM((64, rows), bf16),
                pltpu.VMEM((rows, 128), f32),
                pltpu.VMEM((128, length), f32),
                pltpu.VMEM((length, 128), bf16),
                sems,
            ],
            backward_cost[s],
            grid=(heads,),
            in_specs=[smem]
            + [small] * (2 * heads)
            + [pl.BlockSpec((len(g[0]) * half, 128), lambda i: (0, 0)) for g in scales[s]] * 2
            + [hbm] * (heads + 1),
            out_specs=[small] * heads
            + [hbm] * parts
            + [pl.BlockSpec((16, 128), lambda i: (0, 0))],
            deps=ready,
        )
        ready = [outs[0]]
        if s == seqs - 1:
            act = jnp.concatenate(acts, axis=0) + outs[-1][0, 0]
        zeros.append(outs[-1][0, 0])
        d_got.append((outs[:heads], scatter_blocks(enumerate(outs[heads:-1]), "ctx")))
    sent = []
    for dq, dkv in d_got:
        dkv = dkv + zeros[-1].astype(f32)
        sent.append(
            [
                jnp.concatenate([dkv[h * rows : (h + 1) * rows].astype(bf16), dq[h]], axis=0)
                for h in range(heads)
            ]
        )
    backs = [
        [sent[s][0]] + [swap(sent[s][h], "ctx", h * parts) for h in range(1, heads)] for s in many
    ]
    g_qkv_w = 0.0
    for s in range(seqs):
        back = backs[s]
        outs = call(
            functools.partial(d_qkv_kernel, heads, tp, half),
            [place, *back, w_all, *tables, full1[s]],
            [sds((rows, 3 * every), bf16), sds((1, width), f32)]
            + [sds((own, width), bf16)] * tp,
            [pltpu.VMEM((heads, rows + half, 128), bf16), pltpu.VMEM((rows, width), f32)],
            6,
            deps=[*early, g_qkv_w] if s else sent[1],
        )
        g_qkv_w = g_qkv_w + dot(full1[s], outs[0], 0, 0)
        gain1 = gain1 + outs[1][0]
        _, pull_norm1 = jax.vjp(lambda r: layer_norm(r, norm1_gain), resid[s])
        d_in_norm = pull_norm1(scatter_blocks(enumerate(outs[2:])))[0]
        in_grad.append((d_mid[s] + d_in_norm).astype(bf16))
    orders = [row_order(ctx, turn) for turn in range(2)]
    dealt = call(
        functools.partial(deal_kernel, [o[1] for o in orders]),
        [place, g_qkv_w, g_attn_w],
        [sds((width // 2, 2 * every), bf16)] * 4,
        [],
        3,
    )
    sums = []
    for turn in range(2):
        sums += sum_halves(dealt[2 * turn], dealt[2 * turn + 1], "ctx", orders[turn][0])
    g_qkv_w, g_attn_w = call(
        functools.partial(undeal_kernel, [o[1] for o in orders]),
        [place, *sums],
        [sds((width, 3 * every), f32), sds((width, every), f32)],
        [],
        3,
    )
    g_qkv_w = g_qkv_w.reshape(width, 3, heads, head_dim)

    out_part = dot(act, ffn_out_weight, 1, 0).astype(bf16).reshape(seqs, tp, own, width)
    ffn_sum = scatter_blocks({j: out_part[:, j] for j in range(tp)})
    block_out = (jnp.stack(mid) + ffn_sum).astype(bf16)

    gains = jnp.stack([gain1 / norm1_gain, gain2]) + gate(dealt[0]).astype(f32)
    gains = total(total(gains, "tp"), "ctx")
    return (
        block_out,
        jnp.stack(in_grad),
        gains[0],
        g_qkv_w,
        g_attn_w.T.reshape(heads, head_dim, width),
        gains[1],
        early[0].astype(f32).T.reshape(width, 2, ff),
        early[1].astype(f32),
    )


def solution(mesh):
    in_specs = (
        P(None, ("ctx", "tp"), None),
        P(),
        P(None, None, "tp", None),
        P("tp", None, None),
        P(),
        P(None, None, "tp"),
        P("tp", None),
        P(None, "ctx"),
        P(None, ("ctx", "tp"), None),
    )
    out_specs = (
        P(None, ("ctx", "tp"), None),
        P(None, ("ctx", "tp"), None),
        P(),
        P(None, None, "tp", None),
        P("tp", None, None),
        P(),
        P(None, None, "tp"),
        P("tp", None),
    )
    return jax.shard_map(shards, mesh=mesh, in_specs=in_specs, out_specs=out_specs, check_vma=False)
```

```python
import functools
import math

import jax
import jax.numpy as jnp
from jax import lax
from jax.experimental import pallas as pl
from jax.experimental.pallas import tpu as pltpu
from jax.sharding import PartitionSpec as P

theta_log = math.log(160000.0)
neg_fill = -1e30
safe_bound = 60.0
log2_e = math.log2(math.e)
wide_keys = 1664
fine_keys = 512
cut_count = 4
bf16 = jnp.bfloat16
f32 = jnp.float32
vmem_limit = 56 * 2**20


def swap(block, axis, bits):
    size = lax.axis_size(axis)
    return lax.ppermute(block, axis, [(i, i ^ bits) for i in range(size)])


def bit_list(size):
    bits, b = [], 1
    while b < size:
        bits.append(b)
        b *= 2
    return bits


def total(value, axis):
    for b in bit_list(lax.axis_size(axis)):
        value = value + swap(value, axis, b)
    return value


def gate(array):
    return jnp.minimum(jnp.abs(array[(0,) * array.ndim]), 0)


def gather_blocks(block, axis="tp", bits=None):
    held = {0: block}
    for b in reversed(bit_list(lax.axis_size(axis)) if bits is None else bits):
        for j in list(held):
            held[j ^ b] = swap(held[j], axis, b)
    return [held[j] for j in sorted(held)]


def scatter_blocks(blocks, axis="tp", notes=None):
    held = dict(blocks)
    for b in bit_list(max(held) + 1):
        for j in sorted(held):
            if j & b:
                got = swap(held.pop(j), axis, b)
                summed = held[j ^ b].astype(f32) + got.astype(f32)
                held[j ^ b] = summed if len(held) == 1 else summed.astype(bf16)
        if notes is not None:
            notes.append(list(held.values()))
    return held[0]


def row_order(size, turn):
    bits = bit_list(size)
    bits = bits[turn:] + bits[:turn]
    return bits, sorted(range(size), key=lambda k: [k & b for b in bits])


def sum_halves(keep, send, axis, bits):
    for n, b in enumerate(bits):
        held = (keep.astype(f32) + swap(send, axis, b).astype(f32)).astype(bf16)
        if n < len(bits) - 1:
            mid = held.shape[0] // 2
            keep, send = held[:mid], held[mid:]
    reduced = held
    for b in reversed(bits[1:]):
        held = jnp.concatenate([held, swap(held, axis, b)], axis=0)
    return (held, swap(held, axis, bits[0])), reduced


def dot(a, b, ca, cb):
    return lax.dot_general(a, b, (((ca,), (cb,)), ((), ())), preferred_element_type=f32)


def lanes():
    return lax.broadcasted_iota(jnp.int32, (1, 128), 1)


def rot(u):
    first = (lanes() & 63) < 32
    return jnp.where(first, -pltpu.roll(u, 96, 1), pltpu.roll(u, 32, 1))


def rot_back(w):
    first = (lanes() & 63) < 32
    return jnp.where(first, pltpu.roll(w, 96, 1), -pltpu.roll(w, 32, 1))


def call(
    kernel,
    ins,
    outs,
    scratch,
    cost,
    smem_ins=1,
    grid=None,
    in_specs=None,
    out_specs=None,
    deps=(),
):
    whole = pl.BlockSpec(memory_space=pltpu.VMEM)
    if in_specs is None:
        in_specs = [pl.BlockSpec(memory_space=pltpu.SMEM)] * smem_ins + [whole] * (
            len(ins) - smem_ins
        )
        out_specs = [whole] * len(outs)
    extra = {} if grid is None else {"grid": grid}
    moved = sum(a.size * a.dtype.itemsize for a in [*ins, *outs])
    time = int(cost * 1.15e9)
    used = len(ins)
    ins = [*ins, *deps]
    in_specs = in_specs + [pl.BlockSpec(memory_space=pl.ANY)] * len(deps)

    def body(*refs):
        kernel(*refs[:used], *refs[len(ins) :])

    return pl.pallas_call(
        body,
        in_specs=in_specs,
        out_specs=out_specs,
        out_shape=outs,
        scratch_shapes=scratch,
        compiler_params=pltpu.CompilerParams(vmem_limit_bytes=vmem_limit),
        cost_estimate=pl.CostEstimate(
            flops=time, transcendentals=0, bytes_accessed=int(moved)
        ),
        **extra,
    )(*ins)


def assemble(meta, pieces, x_scr):
    part = pieces[0].shape[0]
    for j, piece in enumerate(pieces):
        at = pl.multiple_of((meta[2] ^ j) * part, 8)
        x_scr[pl.ds(at, part), :] = piece[...].astype(f32)


def disperse(meta, x_scr, pieces):
    part = pieces[0].shape[0]
    for j, piece in enumerate(pieces):
        at = pl.multiple_of((meta[2] ^ j) * part, 8)
        piece[...] = x_scr[pl.ds(at, part), :].astype(bf16)


def pair(u, v):
    return jnp.where(lanes() < 64, u, pltpu.roll(v, 64, 1))


def pair_right(u, v):
    return jnp.where(lanes() < 64, pltpu.roll(u, 64, 1), v)


def qkv_kernel(heads, tp, half, scale, meta, *refs):
    pieces, refs = refs[:tp], refs[tp:]
    weight, cosine, sine, x_ref, zero, *refs = refs
    zero[...] = jnp.zeros_like(zero)
    outs, (x_scr, kv_scr, q_scr) = refs[:heads], refs[heads:]
    assemble(meta, pieces, x_scr)
    x = x_scr[...].astype(bf16)
    x_ref[...] = x
    every = heads * 64
    for t in range(heads // 2):
        q, k, v = [
            dot(x, weight[:, n * every + t * 128 : n * every + (t + 1) * 128], 1, 0)
            for n in range(3)
        ]
        q = (q * cosine[...] + rot(q) * sine[...]) * scale
        k = k * cosine[...] + rot(k) * sine[...]
        kv_scr[2 * t] = pair(k, v).astype(bf16)
        kv_scr[2 * t + 1] = pair_right(k, v).astype(bf16)
        q_scr[2 * t] = pair(q[:half], q[half:]).astype(bf16)
        q_scr[2 * t + 1] = pair_right(q[:half], q[half:]).astype(bf16)
    for kh in range(heads):
        outs[kh][: 2 * half, :] = kv_scr[meta[1] ^ kh]
        outs[kh][2 * half :, :] = q_scr[meta[1] ^ kh]


def row_range(tok, meta, length):
    low = jnp.zeros_like(tok)
    high = jnp.full_like(tok, length)
    for d in range(cut_count):
        c = meta[3 + d]
        low = jnp.where(tok >= c, jnp.maximum(low, c), low)
        high = jnp.where(tok < c, jnp.minimum(high, c), high)
    return low, high


def load_keys(meta, rows, plan, got, kvs, vx, q_scr, sems):
    heads = q_scr.shape[0]
    copies = []
    for c in range(heads):
        source = got[c].at[pl.ds(rows, rows // 2)]
        copies.append(pltpu.make_async_copy(source, q_scr.at[c], sems.at[c]))
    if plan is None:
        copies.append(pltpu.make_async_copy(got[heads], kvs, sems.at[heads]))
    else:
        for n, (ref, start, k) in enumerate(plan):
            at = pl.multiple_of((meta[0] ^ k) * rows, rows)
            source = got[ref].at[pl.ds(start, rows)]
            target = kvs.at[pl.ds(at, rows)]
            copies.append(pltpu.make_async_copy(source, target, sems.at[heads + n]))
    for c in copies:
        c.start()
    for c in copies:
        c.wait()
    vx[...] = jnp.where(lanes() < 64, jnp.ones((), bf16), kvs[...])


def attn_fwd_kernel(heads, ctx, rows, length, count, plan, chosen, meta, *refs):
    got, refs = refs[:count], refs[count:]
    o_refs, refs = refs[: len(chosen)], refs[len(chosen) :]
    linv_ref, m_ref, zero, kv_out, kvs, vx, q_scr, qc, acc, m_scr, norms, sems = refs
    half = rows // 2
    turn = pl.program_id(0)
    i = turn + chosen[0]
    left = lanes() < 64

    @pl.when(turn == 0)
    def _():
        zero[...] = jnp.zeros_like(zero)
        load_keys(meta, rows, plan, got, kvs, vx, q_scr, sems)
        if plan is not None:
            keep = pltpu.make_async_copy(kvs, kv_out, sems.at[0])
            keep.start()
        k = jnp.where(left, kvs[...].astype(f32), 0.0)
        norms[0] = jnp.max(jnp.sum(k * k, axis=1, keepdims=True))
        if plan is not None:
            keep.wait()

    q = q_scr[i].astype(f32)
    qa = jnp.where(left, q, 0.0)
    qb = jnp.where(left, pltpu.roll(q, 64, 1), 0.0)
    qc[:half] = qa.astype(bf16)
    qc[half:] = qb.astype(bf16)
    q_norm = jnp.max(jnp.sum(jnp.maximum(qa * qa, qb * qb), axis=1, keepdims=True))
    safe = q_norm * norms[0] < safe_bound * safe_bound
    single = meta[3] >= length
    fast = jnp.logical_and(safe, single)
    acc[...] = jnp.zeros_like(acc)
    m_scr[...] = jnp.zeros_like(m_scr)

    @pl.when(fast)
    def _():
        def step(j, _):
            keys = pl.ds(pl.multiple_of(j * wide_keys, wide_keys), wide_keys)
            e = jnp.exp2(dot(qc[...], kvs[keys, :], 1, 1)).astype(bf16)
            acc[...] += dot(e, vx[keys, :], 1, 0)
            return 0

        lax.fori_loop(0, length // wide_keys, step, 0)

    @pl.when(jnp.logical_not(fast))
    def _():
        first = (meta[0] ^ (i * (ctx // heads))) * rows
        tok = first + lax.broadcasted_iota(jnp.int32, (rows, 1), 0)
        low, high = row_range(tok, meta, length)
        j_low = lax.div(row_range(first, meta, length)[0], fine_keys)
        j_high = lax.div(row_range(first + rows - 1, meta, length)[1] + fine_keys - 1, fine_keys)

        def masked(j):
            keys = pl.ds(pl.multiple_of(j * fine_keys, fine_keys), fine_keys)
            spot = j * fine_keys + lax.broadcasted_iota(jnp.int32, (1, fine_keys), 1)
            allowed = jnp.logical_and(spot >= low, spot < high)
            return keys, allowed, dot(qc[...], kvs[keys, :], 1, 1)

        @pl.when(jnp.logical_not(safe))
        def _():
            m_scr[...] = jnp.full_like(m_scr, neg_fill)

            def peak(j, _):
                _, allowed, s = masked(j)
                s = jnp.max(jnp.where(allowed, s, neg_fill), axis=1, keepdims=True)
                m_scr[...] = jnp.maximum(m_scr[...], s)
                return 0

            lax.fori_loop(j_low, j_high, peak, 0)

        def step(j, _):
            keys, allowed, s = masked(j)
            e = jnp.where(allowed, jnp.exp2(s - m_scr[:, 0:1]), 0.0).astype(bf16)
            acc[...] += dot(e, vx[keys, :], 1, 0)
            return 0

        lax.fori_loop(j_low, j_high, step, 0)

    a = acc[...]
    o = a / pltpu.roll(a, 64, 1)
    out = jnp.where(left, pltpu.roll(o[:half], 64, 1), o[half:]).astype(bf16)
    for c in range(len(chosen)):

        @pl.when(turn == c)
        def _(c=c):
            o_refs[c][...] = out

    inv = 1.0 / a
    linv_ref[...] = jnp.where(left, inv[:half], pltpu.roll(inv[half:], 64, 1))
    m_ref[...] = jnp.where(left, m_scr[:half], m_scr[half:])


def attn_bwd_kernel(heads, ctx, rows, length, groups, meta, *refs):
    do_refs, refs = refs[:heads], refs[heads:]
    o_refs, refs = refs[:heads], refs[heads:]
    linv_refs, refs = refs[: len(groups)], refs[len(groups) :]
    m_refs, refs = refs[: len(groups)], refs[len(groups) :]
    got, refs = refs[: heads + 1], refs[heads + 1 :]
    dq_refs, refs = refs[:heads], refs[heads:]
    parts = ctx // heads
    dkv_refs, zero, refs = refs[:parts], refs[parts], refs[parts + 1 :]
    kvs, vx, q_scr, do_scr, o_scr, linv_scr, m_scr, *refs = refs
    qc, dc, qt, dt, dq_acc, dkv_t, dkv_n, sems = refs
    half = rows // 2
    i = pl.program_id(0)
    lane = lanes()
    left = lane < 64

    @pl.when(i == 0)
    def _():
        load_keys(meta, rows, None, got, kvs, vx, q_scr, sems)
        zero[...] = jnp.zeros_like(zero)
        dkv_t[...] = jnp.zeros_like(dkv_t)
        for c in range(heads):
            do_scr[c] = do_refs[c][...]
            o_scr[c] = o_refs[c][...]
        for n, g in enumerate(groups):
            side = slice(g[0] * half, (g[-1] + 1) * half)
            linv_scr[side, :] = linv_refs[n][...]
            m_scr[side, :] = m_refs[n][...]

    q = q_scr[i].astype(f32)
    here = pl.ds(pl.multiple_of(i * half, half), half)
    do = do_scr[i].astype(f32) * linv_scr[here, :]
    prod = do * o_scr[i].astype(f32)
    delta_a = jnp.sum(jnp.where(left, prod, 0.0), axis=1, keepdims=True)
    delta_b = jnp.sum(jnp.where(left, 0.0, prod), axis=1, keepdims=True)

    def extended(x, delta):
        coarse = delta.astype(bf16).astype(f32)
        ends = jnp.where(lane == 0, -coarse, jnp.where(lane == 1, coarse - delta, 0.0))
        return jnp.where(left, ends, x).astype(bf16)

    qc[:half] = jnp.where(left, q, 0.0).astype(bf16)
    qc[half:] = jnp.where(left, pltpu.roll(q, 64, 1), 0.0).astype(bf16)
    dc[:half] = extended(pltpu.roll(do, 64, 1), delta_a)
    dc[half:] = extended(do, delta_b)
    qt[...] = qc[...].astype(f32).T[:64].astype(bf16)
    dt[...] = dc[...].astype(f32).T[64:].astype(bf16)
    dq_acc[...] = jnp.zeros_like(dq_acc)
    shift = m_scr[here, :]
    shifted = jnp.max(jnp.abs(shift)) > 0.0
    single = meta[3] >= length
    fast = jnp.logical_and(single, jnp.logical_not(shifted))

    def accumulate(keys, e, allowed):
        ds = e * dot(dc[...], vx[keys, :], 1, 1)
        if allowed is not None:
            ds = jnp.where(allowed, ds, 0.0)
        ds = ds.astype(bf16)
        e = e.astype(bf16)
        dq_acc[...] += dot(ds, kvs[keys, :], 1, 0)
        dkv_t[:64, keys] += dot(qt[...], ds, 1, 0)
        dkv_t[64:, keys] += dot(dt[...], e, 1, 0)

    @pl.when(fast)
    def _():
        def step(j, _):
            keys = pl.ds(pl.multiple_of(j * wide_keys, wide_keys), wide_keys)
            accumulate(keys, jnp.exp2(dot(qc[...], kvs[keys, :], 1, 1)), None)
            return 0

        lax.fori_loop(0, length // wide_keys, step, 0)

    @pl.when(jnp.logical_not(fast))
    def _():
        first = (meta[0] ^ (i * (ctx // heads))) * rows
        tok = first + lax.broadcasted_iota(jnp.int32, (rows, 1), 0)
        low, high = row_range(tok, meta, length)
        j_low = lax.div(row_range(first, meta, length)[0], fine_keys)
        j_high = lax.div(row_range(first + rows - 1, meta, length)[1] + fine_keys - 1, fine_keys)
        m = jnp.concatenate([shift[:, 0:1], shift[:, 64:65]], axis=0)

        def step(j, _):
            keys = pl.ds(pl.multiple_of(j * fine_keys, fine_keys), fine_keys)
            spot = j * fine_keys + lax.broadcasted_iota(jnp.int32, (1, fine_keys), 1)
            allowed = jnp.logical_and(spot >= low, spot < high)
            s = dot(qc[...], kvs[keys, :], 1, 1)
            e = jnp.where(allowed, jnp.exp2(s - m), 0.0)
            accumulate(keys, e, allowed)
            return 0

        lax.fori_loop(j_low, j_high, step, 0)

    a = dq_acc[...] * 0.125
    out = jnp.where(left, a[:half], pltpu.roll(a[half:], 64, 1)).astype(bf16)
    for c in range(heads):

        @pl.when(i == c)
        def _(c=c):
            dq_refs[c][...] = out

    @pl.when(i == heads - 1)
    def _():
        is_key = lax.broadcasted_iota(jnp.int32, (128, 1), 0) < 64
        for j in range(length // wide_keys):
            part = dkv_t[:, j * wide_keys : (j + 1) * wide_keys]
            part = jnp.where(is_key, part * math.log(2.0), part)
            dkv_n[j * wide_keys : (j + 1) * wide_keys, :] = part.T.astype(bf16)
        copies = []
        for k in range(ctx):
            at = pl.multiple_of((meta[0] ^ k) * rows, rows)
            target = dkv_refs[k % parts].at[pl.ds(k // parts * rows, rows)]
            copies.append(pltpu.make_async_copy(dkv_n.at[pl.ds(at, rows)], target, sems.at[k]))
        for c in copies:
            c.start()
        for c in copies:
            c.wait()


def proj_kernel(heads, tp, meta, *refs):
    o_refs, refs = refs[:heads], refs[heads:]
    weight, o_nat, *refs = refs
    pieces, (o_scr, x_scr) = refs[:tp], refs[tp:]
    half = o_refs[0].shape[0]
    for kh in range(heads):
        o_scr[meta[1] ^ kh] = o_refs[kh][...]
    for t in range(heads // 2):
        u, v = o_scr[2 * t].astype(f32), o_scr[2 * t + 1].astype(f32)
        o_nat[:half, t * 128 : (t + 1) * 128] = pair(u, v).astype(bf16)
        o_nat[half:, t * 128 : (t + 1) * 128] = pair_right(u, v).astype(bf16)
    x_scr[...] = dot(o_nat[...], weight[...], 1, 0)
    disperse(meta, x_scr, pieces)


def d_attn_kernel(heads, tp, meta, *refs):
    pieces, refs = refs[:tp], refs[tp:]
    weight, full, zero, *refs = refs
    zero[...] = jnp.zeros_like(zero)
    outs, (x_scr, d_scr) = refs[:heads], refs[heads:]
    half = outs[0].shape[0]
    assemble(meta, pieces, x_scr)
    x = x_scr[...].astype(bf16)
    full[...] = x
    for t in range(heads // 2):
        d = dot(x, weight[t * 128 : (t + 1) * 128, :], 1, 1)
        d_scr[2 * t] = pair(d[:half], d[half:]).astype(bf16)
        d_scr[2 * t + 1] = pair_right(d[:half], d[half:]).astype(bf16)
    for kh in range(heads):
        outs[kh][...] = d_scr[meta[1] ^ kh]


def d_qkv_kernel(heads, tp, half, meta, *refs):
    got, refs = refs[:heads], refs[heads:]
    weight, cosine, sine, normed, d_all, gain, *refs = refs
    pieces, (scr, x_scr) = refs[:tp], refs[tp:]
    every = heads * 64
    for kh in range(heads):
        scr[meta[1] ^ kh] = got[kh][...]
    for t in range(heads // 2):
        u, v = scr[2 * t].astype(f32), scr[2 * t + 1].astype(f32)
        dk, dv = pair(u[: 2 * half], v[: 2 * half]), pair_right(u[: 2 * half], v[: 2 * half])
        u, v = u[2 * half :], v[2 * half :]
        dq = jnp.concatenate([pair(u, v), pair_right(u, v)], axis=0)
        dq = dq * cosine[...] + rot_back(dq * sine[...])
        dk = dk * cosine[...] + rot_back(dk * sine[...])
        for n, d in enumerate((dq, dk, dv)):
            d_all[:, n * every + t * 128 : n * every + (t + 1) * 128] = d.astype(bf16)
    x_scr[...] = dot(d_all[...], weight[...], 1, 1)
    gain[...] = jnp.sum(x_scr[...] * normed[...].astype(f32), axis=0, keepdims=True)
    disperse(meta, x_scr, pieces)


def deal_kernel(orders, meta, grad, other, *outs):
    part, wide = grad.shape[0] // len(orders[0]), outs[0].shape[1]
    split = grad.shape[1] - wide
    deep = len(orders[0]) // 2
    for c, order in enumerate(orders):
        for n, k in enumerate(order):
            at = pl.ds(pl.multiple_of((meta[0] ^ k) * part, part), part)
            out, place = outs[2 * c + n // deep], pl.ds(n % deep * part, part)
            if c == 0:
                out[place, :] = grad[at, :wide].astype(bf16)
            else:
                out[place, :split] = grad[at, wide:].astype(bf16)
                out[place, split:] = other[at, :].astype(bf16)


def undeal_kernel(orders, meta, *refs):
    ins, (grad, other) = refs[:4], refs[4:]
    part, wide = grad.shape[0] // len(orders[0]), ins[0].shape[1]
    split = grad.shape[1] - wide
    deep = len(orders[0]) // 2
    for c, order in enumerate(orders):
        for n, k in enumerate(order):
            at = pl.ds(pl.multiple_of((meta[0] ^ k) * part, part), part)
            block = ins[2 * c + n // deep][n % deep * part : (n % deep + 1) * part, :].astype(f32)
            if c == 0:
                grad[at, :wide] = block
            else:
                grad[at, wide:] = block[:, :split]
                other[at, :] = block[:, split:]


def rope_tables(positions, width):
    freqs = jnp.exp(-(2.0 * jnp.arange(width // 2, dtype=f32) / width) * theta_log)
    angles = positions.astype(f32)[:, None] * freqs[None, :]
    cosine, sine = jnp.cos(angles), jnp.sin(angles)
    lay = lambda u: jnp.concatenate([u, u, u, u], axis=1)
    return lay(cosine), lay(sine)


def layer_norm(rows, gain):
    mean = jnp.mean(rows, axis=-1, keepdims=True)
    cent = rows - mean
    var = jnp.mean(cent * cent, axis=-1, keepdims=True)
    return cent * lax.rsqrt(var + 1e-05) * gain


def shards(
    hidden_in,
    norm1_gain,
    qkv_weight,
    attn_weight,
    norm2_gain,
    ffn_in_weight,
    ffn_out_weight,
    doc_ids,
    out_grad,
):
    seqs = hidden_in.shape[0]
    width = hidden_in.shape[2]
    heads = qkv_weight.shape[2]
    head_dim = qkv_weight.shape[3]
    rows = doc_ids.shape[1]
    half = rows // 2
    ff = ffn_out_weight.shape[0]
    ctx, tp = lax.axis_size("ctx"), lax.axis_size("tp")
    parts = ctx // heads
    length = ctx * rows
    own = rows // tp
    me, spot = lax.axis_index("ctx"), lax.axis_index("tp")
    sds = jax.ShapeDtypeStruct

    steps = jnp.arange(1, cut_count + 1, dtype=jnp.int32)
    counts = jnp.sum((doc_ids[:, :, None] < steps).astype(f32), axis=1)
    cuts = total(counts, "ctx").astype(jnp.int32)
    place = jnp.stack([me, me // parts, spot]).astype(jnp.int32)
    metas = [jnp.concatenate([place, cuts[s]]) for s in range(seqs)]

    every = heads * head_dim
    w_all = qkv_weight.reshape(width, 3 * every)
    w_out = attn_weight.reshape(every, width)
    w_in = ffn_in_weight.reshape(width, 2 * ff)
    tables = rope_tables(me * rows + jnp.arange(rows, dtype=jnp.int32), head_dim)
    scale = log2_e / math.sqrt(head_dim)

    resid = [hidden_in[s].astype(f32) for s in range(seqs)]
    full1, sents, mines = [], [], []

    def spread(s, zero):
        mine = mines[s]
        rest = jnp.concatenate([m[:rows] for m in mine], axis=0) + zero
        held = [(rest, [h * parts for h in range(heads)])]
        plan = [(h, 0, h * parts) for h in range(heads)]
        arrays = list(mine)
        for b in bit_list(parts):
            for block, ks in list(held):
                ks = [k ^ b for k in ks]
                held.append((swap(block, "ctx", b), ks))
                plan += [(len(arrays), n * rows, k) for n, k in enumerate(ks)]
                arrays.append(held[-1][0])
        return arrays, rest, plan

    for s in range(seqs):
        blocks = gather_blocks(layer_norm(resid[s], norm1_gain).astype(bf16))
        outs = call(
            functools.partial(qkv_kernel, heads, tp, half, scale),
            [place, *blocks, w_all, *tables],
            [sds((rows, width), bf16), sds((16, 128), bf16)]
            + [sds((rows + half, 128), bf16)] * heads,
            [
                pltpu.VMEM((rows, width), f32),
                pltpu.VMEM((heads, rows, 128), bf16),
                pltpu.VMEM((heads, half, 128), bf16),
            ],
            7,
            deps=[got[0][1]] if s else [cuts],
        )
        full1.append(outs[0])
        sent = outs[2:]
        sents.append(sent)
        sent_zero = outs[1][0, 0]
        mines.append([sent[0]] + [swap(sent[h], "ctx", h * parts) for h in range(1, heads)])
        if s == 0:
            got = [spread(0, jnp.zeros((), bf16))]

    smem = pl.BlockSpec(memory_space=pltpu.SMEM)
    hbm = pl.BlockSpec(memory_space=pl.ANY)
    small = pl.BlockSpec((half, 128), lambda i: (0, 0))
    tile = pl.BlockSpec((half, 128), lambda i: (i, 0))
    key_scratch = [
        pltpu.VMEM((length, 128), bf16),
        pltpu.VMEM((length, 128), bf16),
        pltpu.VMEM((heads, half, 128), bf16),
    ]
    sems = pltpu.SemaphoreType.DMA((ctx + heads,))

    def attend(s, chosen, deps):
        first = kept[s] is None
        ins = got[s][0] if first else [*mines[s], kept[s]]
        tiles = len(chosen)
        outs = call(
            functools.partial(
                attn_fwd_kernel, heads, ctx, rows, length, len(ins), plan if first else None, chosen
            ),
            [metas[s], *ins],
            [sds((half, 128), bf16)] * tiles
            + [sds((tiles * half, 128), f32)] * 2
            + [sds((8, 128), f32), sds((length if first else 16, 128), bf16)],
            key_scratch
            + [
                pltpu.VMEM((rows, 128), bf16),
                pltpu.VMEM((rows, 128), f32),
                pltpu.VMEM((rows, 128), f32),
                pltpu.SMEM((1,), f32),
                sems,
            ],
            2 + 9 * tiles * length / 6656,
            grid=(tiles,),
            in_specs=[smem] + [hbm] * len(ins),
            out_specs=[small] * tiles
            + [tile, tile, pl.BlockSpec((8, 128), lambda i: (0, 0)), hbm],
            deps=deps,
        )
        if first:
            kept[s] = outs[tiles + 3]
        for n, h in enumerate(chosen):
            o_mine[s][h] = outs[n]
            back[s][h] = outs[n] if h == 0 else swap(outs[n], "ctx", h * parts)
        scales[s].append((chosen, outs[tiles], outs[tiles + 1]))
        return outs[tiles + 2]

    def project(s, deps, notes):
        outs = call(
            functools.partial(proj_kernel, heads, tp),
            [place, *[back[s][h] for h in range(heads)], w_out],
            [sds((rows, every), bf16)] + [sds((own, width), bf16)] * tp,
            [pltpu.VMEM((heads, half, 128), bf16), pltpu.VMEM((rows, width), f32)],
            3,
            deps=deps,
        )
        o_nat[s] = outs[0]
        mid[s] = resid[s] + scatter_blocks(enumerate(outs[1:]), "tp", notes)

    def second_norm(s, zero):
        normed, pull_norm2[s] = jax.vjp(layer_norm, mid[s] + zero, norm2_gain)
        normed = normed.astype(bf16)
        blocks = gather_blocks(normed)
        full2[s] = jnp.concatenate(blocks, axis=0)
        return normed, blocks[2]

    many = range(seqs)
    kept, o_nat, mid = [None] * seqs, [None] * seqs, [None] * seqs
    full2, pull_norm2 = [None] * seqs, [None] * seqs
    o_mine, back, scales = [{} for _ in many], [{} for _ in many], [[] for _ in many]
    plan = got[0][2]
    grads_all = (out_grad + sent_zero).reshape(seqs * own, width)
    grad_blocks = gather_blocks(grads_all)
    grads_all = jnp.concatenate(grad_blocks, axis=0).reshape(tp, seqs, own, width)
    grads_all = grads_all.transpose(1, 0, 2, 3).reshape(seqs * rows, width)
    got.append(spread(1, jnp.zeros((), bf16)))
    mark = attend(0, list(range(heads)), [got[1][1], grad_blocks[2]])
    mark = attend(1, list(range(heads - 1, heads)), [mark])
    notes = []
    project(0, [mark], notes)
    waits = [notes[0][0]]
    for n, h in enumerate(reversed(range(heads - 1))):
        mark = attend(1, [h], [mark, *waits])
        if n == 0:
            waits = second_norm(0, mark[0, 0])
            waits, later = [waits[0]], [waits[1]]
        else:
            waits, later = later, []
    notes = []
    project(1, [mark], notes)
    full2[0] = full2[0] + gate(notes[0][0])
    last_rows = second_norm(1, 0.0)[1]

    acts, d_mid, d_pieces, gain2 = [], [], [], 0.0

    def to_heads(s, deps):
        outs = call(
            functools.partial(d_attn_kernel, heads, tp),
            [place, *d_pieces[s], w_out],
            [sds((rows, width), bf16), sds((16, 128), bf16)] + [sds((half, 128), bf16)] * heads,
            [pltpu.VMEM((rows, width), f32), pltpu.VMEM((heads, half, 128), bf16)],
            4,
            deps=deps,
        )
        d = outs[2:]
        d = [d[0]] + [swap(d[h], "ctx", h * parts) for h in range(1, heads)]
        return outs[0], d, outs[1][0, 0]

    zero = gate(last_rows)
    g_out_w, g_in_w = 0.0, 0.0
    for s in range(seqs):
        upper = dot(full2[s], w_in, 1, 0)
        grads = grads_all[s * rows : (s + 1) * rows]
        gated, pull_gelu = jax.vjp(
            lambda a, b: jax.nn.gelu(a, approximate=False) * b, upper[:, :ff], upper[:, ff:]
        )
        act = gated.astype(bf16)
        d_act = dot(grads, ffn_out_weight, 1, 1)
        d_upper = jnp.concatenate(pull_gelu(d_act), axis=1).astype(bf16)
        d_part = dot(d_upper + zero, w_in, 1, 1).astype(bf16)
        notes = []
        d_normed2 = scatter_blocks(
            {j: d_part[j * own : (j + 1) * own] for j in range(tp)}, "tp", notes
        )
        g_out_w = g_out_w + dot(act, grads, 0, 0)
        g_in_w = g_in_w + dot(d_upper, full2[s], 0, 0)
        if s == seqs - 1:
            g_in_w = g_in_w.astype(bf16)
            d_normed2 = d_normed2 + gate(g_in_w).astype(f32)
        d_mid_norm, d_gain = pull_norm2[s](d_normed2)
        gain2 = gain2 + d_gain
        d_mid.append(out_grad[s].astype(f32) + d_mid_norm)
        d_pieces.append(gather_blocks(d_mid[s].astype(bf16)))
        if s == 0:
            dmid_full, d_attn, zero = to_heads(0, [g_in_w, g_out_w])
            g_attn_w = dot(dmid_full, o_nat[0], 0, 0)
        acts.append(act)
    later_dmid, later_attn, _ = to_heads(1, [])
    d_attns = [d_attn, later_attn]
    g_attn_w = g_attn_w + dot(later_dmid, o_nat[1], 0, 0)
    g_out_w = g_out_w + gate(d_attn[heads - 1]).astype(f32)
    ready = [g.astype(bf16) for g in (g_in_w, g_out_w)]
    early = lax.psum(ready, "ctx")
    ready = [g[:16, :128] for g in ready] + [later_dmid]

    in_grad, gain1, zeros, d_got = [], 0.0, [], []
    backward_cost = [1, 1]
    for s in range(seqs):
        outs = call(
            functools.partial(
                attn_bwd_kernel, heads, ctx, rows, length, [g[0] for g in scales[s]]
            ),
            [
                metas[s],
                *d_attns[s],
                *[o_mine[s][h] for h in range(heads)],
                *[g[1] for g in scales[s]],
                *[g[2] for g in scales[s]],
                *mines[s],
                kept[s],
            ],
            [sds((half, 128), bf16)] * heads
            + [sds((heads * rows, 128), bf16)] * parts
            + [sds((16, 128), bf16)],
            key_scratch
            + [
                pltpu.VMEM((heads, half, 128), bf16),
                pltpu.VMEM((heads, half, 128), bf16),
                pltpu.VMEM((heads * half, 128), f32),
                pltpu.VMEM((heads * half, 128), f32),
                pltpu.VMEM((rows, 128), bf16),
                pltpu.VMEM((rows, 128), bf16),
                pltpu.VMEM((64, rows), bf16),
                pltpu.VMEM((64, rows), bf16),
                pltpu.VMEM((rows, 128), f32),
                pltpu.VMEM((128, length), f32),
                pltpu.VMEM((length, 128), bf16),
                sems,
            ],
            backward_cost[s],
            grid=(heads,),
            in_specs=[smem]
            + [small] * (2 * heads)
            + [pl.BlockSpec((len(g[0]) * half, 128), lambda i: (0, 0)) for g in scales[s]] * 2
            + [hbm] * (heads + 1),
            out_specs=[small] * heads
            + [hbm] * parts
            + [pl.BlockSpec((16, 128), lambda i: (0, 0))],
            deps=ready,
        )
        ready = [outs[0]]
        if s == seqs - 1:
            act = jnp.concatenate(acts, axis=0) + outs[-1][0, 0]
        zeros.append(outs[-1][0, 0])
        d_got.append((outs[:heads], scatter_blocks(enumerate(outs[heads:-1]), "ctx")))
    sent = []
    for dq, dkv in d_got:
        dkv = dkv + zeros[-1].astype(f32)
        sent.append(
            [
                jnp.concatenate([dkv[h * rows : (h + 1) * rows].astype(bf16), dq[h]], axis=0)
                for h in range(heads)
            ]
        )
    backs = [
        [sent[s][0]] + [swap(sent[s][h], "ctx", h * parts) for h in range(1, heads)] for s in many
    ]
    out_part = dot(act, ffn_out_weight, 1, 0).astype(bf16).reshape(seqs, tp, own, width)
    ffn_sum = scatter_blocks({j: out_part[:, j] for j in range(tp)})
    block_out = (jnp.stack(mid) + ffn_sum).astype(bf16)

    g_qkv_w = 0.0
    for s in range(seqs):
        back = backs[s]
        outs = call(
            functools.partial(d_qkv_kernel, heads, tp, half),
            [place, *back, w_all, *tables, full1[s]],
            [sds((rows, 3 * every), bf16), sds((1, width), f32)]
            + [sds((own, width), bf16)] * tp,
            [pltpu.VMEM((heads, rows + half, 128), bf16), pltpu.VMEM((rows, width), f32)],
            6,
            deps=[*early, g_qkv_w, in_grad[0]] if s else [*sent[1], block_out],
        )
        g_qkv_w = g_qkv_w + dot(full1[s], outs[0], 0, 0)
        gain1 = gain1 + outs[1][0]
        _, pull_norm1 = jax.vjp(lambda r: layer_norm(r, norm1_gain), resid[s])
        d_in_norm = pull_norm1(scatter_blocks(enumerate(outs[2:])))[0]
        in_grad.append((d_mid[s] + d_in_norm).astype(bf16))
    orders = [row_order(ctx, turn) for turn in range(2)]
    dealt = call(
        functools.partial(deal_kernel, [o[1] for o in orders]),
        [place, g_qkv_w, g_attn_w],
        [sds((width // 2, 2 * every), bf16)] * 4,
        [],
        3,
    )
    sums = []
    for turn in range(2):
        ends, reduced = sum_halves(dealt[2 * turn], dealt[2 * turn + 1], "ctx", orders[turn][0])
        sums += ends
    g_qkv_w, g_attn_w = call(
        functools.partial(undeal_kernel, [o[1] for o in orders]),
        [place, *sums],
        [sds((width, 3 * every), f32), sds((width, every), f32)],
        [],
        3,
    )
    g_qkv_w = g_qkv_w.reshape(width, 3, heads, head_dim)

    gains = jnp.stack([gain1 / norm1_gain, gain2]) + gate(reduced).astype(f32)
    gains = total(total(gains, "tp"), "ctx")
    return (
        block_out,
        jnp.stack(in_grad),
        gains[0],
        g_qkv_w,
        g_attn_w.T.reshape(heads, head_dim, width),
        gains[1],
        early[0].astype(f32).T.reshape(width, 2, ff),
        early[1].astype(f32),
    )


def solution(mesh):
    in_specs = (
        P(None, ("ctx", "tp"), None),
        P(),
        P(None, None, "tp", None),
        P("tp", None, None),
        P(),
        P(None, None, "tp"),
        P("tp", None),
        P(None, "ctx"),
        P(None, ("ctx", "tp"), None),
    )
    out_specs = (
        P(None, ("ctx", "tp"), None),
        P(None, ("ctx", "tp"), None),
        P(),
        P(None, None, "tp", None),
        P("tp", None, None),
        P(),
        P(None, None, "tp"),
        P("tp", None),
    )
    return jax.shard_map(shards, mesh=mesh, in_specs=in_specs, out_specs=out_specs, check_vma=False)
```

```python
import functools
import math

import jax
import jax.numpy as jnp
from jax import lax
from jax.experimental import pallas as pl
from jax.experimental.pallas import tpu as pltpu
from jax.sharding import PartitionSpec as P

theta_log = math.log(160000.0)
neg_fill = -1e30
safe_bound = 60.0
log2_e = math.log2(math.e)
wide_keys = 1664
fine_keys = 512
cut_count = 4
bf16 = jnp.bfloat16
f32 = jnp.float32
vmem_limit = 56 * 2**20


def swap(block, axis, bits):
    size = lax.axis_size(axis)
    return lax.ppermute(block, axis, [(i, i ^ bits) for i in range(size)])


def bit_list(size):
    bits, b = [], 1
    while b < size:
        bits.append(b)
        b *= 2
    return bits


def total(value, axis):
    for b in bit_list(lax.axis_size(axis)):
        value = value + swap(value, axis, b)
    return value


def gate(array):
    return jnp.minimum(jnp.abs(array[(0,) * array.ndim]), 0)


def gather_blocks(block, axis="tp", bits=None):
    held = {0: block}
    for b in reversed(bit_list(lax.axis_size(axis)) if bits is None else bits):
        for j in list(held):
            held[j ^ b] = swap(held[j], axis, b)
    return [held[j] for j in sorted(held)]


def scatter_blocks(blocks, axis="tp", notes=None):
    held = dict(blocks)
    for b in bit_list(max(held) + 1):
        for j in sorted(held):
            if j & b:
                got = swap(held.pop(j), axis, b)
                summed = held[j ^ b].astype(f32) + got.astype(f32)
                held[j ^ b] = summed if len(held) == 1 else summed.astype(bf16)
        if notes is not None:
            notes.append(list(held.values()))
    return held[0]


def row_order(size, turn):
    bits = bit_list(size)
    bits = bits[turn:] + bits[:turn]
    return bits, sorted(range(size), key=lambda k: [k & b for b in bits])


def sum_halves(keep, send, axis, bits):
    for n, b in enumerate(bits):
        held = (keep.astype(f32) + swap(send, axis, b).astype(f32)).astype(bf16)
        if n < len(bits) - 1:
            mid = held.shape[0] // 2
            keep, send = held[:mid], held[mid:]
    reduced = held
    for b in reversed(bits[1:]):
        held = jnp.concatenate([held, swap(held, axis, b)], axis=0)
    return (held, swap(held, axis, bits[0])), reduced


def dot(a, b, ca, cb):
    return lax.dot_general(a, b, (((ca,), (cb,)), ((), ())), preferred_element_type=f32)


def lanes():
    return lax.broadcasted_iota(jnp.int32, (1, 128), 1)


def rot(u):
    first = (lanes() & 63) < 32
    return jnp.where(first, -pltpu.roll(u, 96, 1), pltpu.roll(u, 32, 1))


def rot_back(w):
    first = (lanes() & 63) < 32
    return jnp.where(first, pltpu.roll(w, 96, 1), -pltpu.roll(w, 32, 1))


def call(
    kernel,
    ins,
    outs,
    scratch,
    cost,
    smem_ins=1,
    grid=None,
    in_specs=None,
    out_specs=None,
    deps=(),
):
    whole = pl.BlockSpec(memory_space=pltpu.VMEM)
    if in_specs is None:
        in_specs = [pl.BlockSpec(memory_space=pltpu.SMEM)] * smem_ins + [whole] * (
            len(ins) - smem_ins
        )
        out_specs = [whole] * len(outs)
    extra = {} if grid is None else {"grid": grid}
    moved = sum(a.size * a.dtype.itemsize for a in [*ins, *outs])
    time = int(cost * 1.15e9)
    used = len(ins)
    ins = [*ins, *deps]
    in_specs = in_specs + [pl.BlockSpec(memory_space=pl.ANY)] * len(deps)

    def body(*refs):
        kernel(*refs[:used], *refs[len(ins) :])

    return pl.pallas_call(
        body,
        in_specs=in_specs,
        out_specs=out_specs,
        out_shape=outs,
        scratch_shapes=scratch,
        compiler_params=pltpu.CompilerParams(vmem_limit_bytes=vmem_limit),
        cost_estimate=pl.CostEstimate(
            flops=time, transcendentals=0, bytes_accessed=int(moved)
        ),
        **extra,
    )(*ins)


def assemble(meta, pieces, x_scr):
    part = pieces[0].shape[0]
    for j, piece in enumerate(pieces):
        at = pl.multiple_of((meta[2] ^ j) * part, 8)
        x_scr[pl.ds(at, part), :] = piece[...].astype(f32)


def disperse(meta, x_scr, pieces):
    part = pieces[0].shape[0]
    for j, piece in enumerate(pieces):
        at = pl.multiple_of((meta[2] ^ j) * part, 8)
        piece[...] = x_scr[pl.ds(at, part), :].astype(bf16)


def pair(u, v):
    return jnp.where(lanes() < 64, u, pltpu.roll(v, 64, 1))


def pair_right(u, v):
    return jnp.where(lanes() < 64, pltpu.roll(u, 64, 1), v)


def qkv_kernel(heads, tp, half, scale, meta, *refs):
    pieces, refs = refs[:tp], refs[tp:]
    weight, cosine, sine, x_ref, zero, *refs = refs
    zero[...] = jnp.zeros_like(zero)
    outs, (x_scr, kv_scr, q_scr) = refs[:heads], refs[heads:]
    assemble(meta, pieces, x_scr)
    x = x_scr[...].astype(bf16)
    x_ref[...] = x
    every = heads * 64
    for t in range(heads // 2):
        q, k, v = [
            dot(x, weight[:, n * every + t * 128 : n * every + (t + 1) * 128], 1, 0)
            for n in range(3)
        ]
        q = (q * cosine[...] + rot(q) * sine[...]) * scale
        k = k * cosine[...] + rot(k) * sine[...]
        kv_scr[2 * t] = pair(k, v).astype(bf16)
        kv_scr[2 * t + 1] = pair_right(k, v).astype(bf16)
        q_scr[2 * t] = pair(q[:half], q[half:]).astype(bf16)
        q_scr[2 * t + 1] = pair_right(q[:half], q[half:]).astype(bf16)
    for kh in range(heads):
        outs[kh][: 2 * half, :] = kv_scr[meta[1] ^ kh]
        outs[kh][2 * half :, :] = q_scr[meta[1] ^ kh]


def row_range(tok, meta, length):
    low = jnp.zeros_like(tok)
    high = jnp.full_like(tok, length)
    for d in range(cut_count):
        c = meta[3 + d]
        low = jnp.where(tok >= c, jnp.maximum(low, c), low)
        high = jnp.where(tok < c, jnp.minimum(high, c), high)
    return low, high


def load_keys(meta, rows, plan, got, kvs, vx, q_scr, sems):
    heads = q_scr.shape[0]
    copies = []
    for c in range(heads):
        source = got[c].at[pl.ds(rows, rows // 2)]
        copies.append(pltpu.make_async_copy(source, q_scr.at[c], sems.at[c]))
    if plan is None:
        copies.append(pltpu.make_async_copy(got[heads], kvs, sems.at[heads]))
    else:
        for n, (ref, start, k) in enumerate(plan):
            at = pl.multiple_of((meta[0] ^ k) * rows, rows)
            source = got[ref].at[pl.ds(start, rows)]
            target = kvs.at[pl.ds(at, rows)]
            copies.append(pltpu.make_async_copy(source, target, sems.at[heads + n]))
    for c in copies:
        c.start()
    for c in copies:
        c.wait()
    vx[...] = jnp.where(lanes() < 64, jnp.ones((), bf16), kvs[...])


def attn_fwd_kernel(heads, ctx, rows, length, count, plan, chosen, meta, *refs):
    got, refs = refs[:count], refs[count:]
    o_refs, refs = refs[: len(chosen)], refs[len(chosen) :]
    linv_ref, m_ref, zero, kv_out, kvs, vx, q_scr, qc, acc, m_scr, norms, sems = refs
    half = rows // 2
    turn = pl.program_id(0)
    i = turn + chosen[0]
    left = lanes() < 64

    @pl.when(turn == 0)
    def _():
        zero[...] = jnp.zeros_like(zero)
        load_keys(meta, rows, plan, got, kvs, vx, q_scr, sems)
        if plan is not None:
            keep = pltpu.make_async_copy(kvs, kv_out, sems.at[0])
            keep.start()
        k = jnp.where(left, kvs[...].astype(f32), 0.0)
        norms[0] = jnp.max(jnp.sum(k * k, axis=1, keepdims=True))
        if plan is not None:
            keep.wait()

    q = q_scr[i].astype(f32)
    qa = jnp.where(left, q, 0.0)
    qb = jnp.where(left, pltpu.roll(q, 64, 1), 0.0)
    qc[:half] = qa.astype(bf16)
    qc[half:] = qb.astype(bf16)
    q_norm = jnp.max(jnp.sum(jnp.maximum(qa * qa, qb * qb), axis=1, keepdims=True))
    safe = q_norm * norms[0] < safe_bound * safe_bound
    single = meta[3] >= length
    fast = jnp.logical_and(safe, single)
    acc[...] = jnp.zeros_like(acc)
    m_scr[...] = jnp.zeros_like(m_scr)

    @pl.when(fast)
    def _():
        def step(j, _):
            keys = pl.ds(pl.multiple_of(j * wide_keys, wide_keys), wide_keys)
            e = jnp.exp2(dot(qc[...], kvs[keys, :], 1, 1)).astype(bf16)
            acc[...] += dot(e, vx[keys, :], 1, 0)
            return 0

        lax.fori_loop(0, length // wide_keys, step, 0)

    @pl.when(jnp.logical_not(fast))
    def _():
        first = (meta[0] ^ (i * (ctx // heads))) * rows
        tok = first + lax.broadcasted_iota(jnp.int32, (rows, 1), 0)
        low, high = row_range(tok, meta, length)
        j_low = lax.div(row_range(first, meta, length)[0], fine_keys)
        j_high = lax.div(row_range(first + rows - 1, meta, length)[1] + fine_keys - 1, fine_keys)

        def masked(j):
            keys = pl.ds(pl.multiple_of(j * fine_keys, fine_keys), fine_keys)
            spot = j * fine_keys + lax.broadcasted_iota(jnp.int32, (1, fine_keys), 1)
            allowed = jnp.logical_and(spot >= low, spot < high)
            return keys, allowed, dot(qc[...], kvs[keys, :], 1, 1)

        @pl.when(jnp.logical_not(safe))
        def _():
            m_scr[...] = jnp.full_like(m_scr, neg_fill)

            def peak(j, _):
                _, allowed, s = masked(j)
                s = jnp.max(jnp.where(allowed, s, neg_fill), axis=1, keepdims=True)
                m_scr[...] = jnp.maximum(m_scr[...], s)
                return 0

            lax.fori_loop(j_low, j_high, peak, 0)

        def step(j, _):
            keys, allowed, s = masked(j)
            e = jnp.where(allowed, jnp.exp2(s - m_scr[:, 0:1]), 0.0).astype(bf16)
            acc[...] += dot(e, vx[keys, :], 1, 0)
            return 0

        lax.fori_loop(j_low, j_high, step, 0)

    a = acc[...]
    o = a / pltpu.roll(a, 64, 1)
    out = jnp.where(left, pltpu.roll(o[:half], 64, 1), o[half:]).astype(bf16)
    for c in range(len(chosen)):

        @pl.when(turn == c)
        def _(c=c):
            o_refs[c][...] = out

    inv = 1.0 / a
    linv_ref[...] = jnp.where(left, inv[:half], pltpu.roll(inv[half:], 64, 1))
    m_ref[...] = jnp.where(left, m_scr[:half], m_scr[half:])


def attn_bwd_kernel(heads, ctx, rows, length, groups, meta, *refs):
    do_refs, refs = refs[:heads], refs[heads:]
    o_refs, refs = refs[:heads], refs[heads:]
    linv_refs, refs = refs[: len(groups)], refs[len(groups) :]
    m_refs, refs = refs[: len(groups)], refs[len(groups) :]
    got, refs = refs[: heads + 1], refs[heads + 1 :]
    dq_refs, refs = refs[:heads], refs[heads:]
    parts = ctx // heads
    dkv_refs, zero, refs = refs[:parts], refs[parts], refs[parts + 1 :]
    kvs, vx, q_scr, do_scr, o_scr, linv_scr, m_scr, *refs = refs
    qc, dc, qt, dt, dq_acc, dkv_t, dkv_n, sems = refs
    half = rows // 2
    i = pl.program_id(0)
    lane = lanes()
    left = lane < 64

    @pl.when(i == 0)
    def _():
        load_keys(meta, rows, None, got, kvs, vx, q_scr, sems)
        zero[...] = jnp.zeros_like(zero)
        dkv_t[...] = jnp.zeros_like(dkv_t)
        for c in range(heads):
            do_scr[c] = do_refs[c][...]
            o_scr[c] = o_refs[c][...]
        for n, g in enumerate(groups):
            side = slice(g[0] * half, (g[-1] + 1) * half)
            linv_scr[side, :] = linv_refs[n][...]
            m_scr[side, :] = m_refs[n][...]

    q = q_scr[i].astype(f32)
    here = pl.ds(pl.multiple_of(i * half, half), half)
    do = do_scr[i].astype(f32) * linv_scr[here, :]
    prod = do * o_scr[i].astype(f32)
    delta_a = jnp.sum(jnp.where(left, prod, 0.0), axis=1, keepdims=True)
    delta_b = jnp.sum(jnp.where(left, 0.0, prod), axis=1, keepdims=True)

    def extended(x, delta):
        coarse = delta.astype(bf16).astype(f32)
        ends = jnp.where(lane == 0, -coarse, jnp.where(lane == 1, coarse - delta, 0.0))
        return jnp.where(left, ends, x).astype(bf16)

    qc[:half] = jnp.where(left, q, 0.0).astype(bf16)
    qc[half:] = jnp.where(left, pltpu.roll(q, 64, 1), 0.0).astype(bf16)
    dc[:half] = extended(pltpu.roll(do, 64, 1), delta_a)
    dc[half:] = extended(do, delta_b)
    qt[...] = qc[...].astype(f32).T[:64].astype(bf16)
    dt[...] = dc[...].astype(f32).T[64:].astype(bf16)
    dq_acc[...] = jnp.zeros_like(dq_acc)
    shift = m_scr[here, :]
    shifted = jnp.max(jnp.abs(shift)) > 0.0
    single = meta[3] >= length
    fast = jnp.logical_and(single, jnp.logical_not(shifted))

    def accumulate(keys, e, allowed):
        ds = e * dot(dc[...], vx[keys, :], 1, 1)
        if allowed is not None:
            ds = jnp.where(allowed, ds, 0.0)
        ds = ds.astype(bf16)
        e = e.astype(bf16)
        dq_acc[...] += dot(ds, kvs[keys, :], 1, 0)
        dkv_t[:64, keys] += dot(qt[...], ds, 1, 0)
        dkv_t[64:, keys] += dot(dt[...], e, 1, 0)

    @pl.when(fast)
    def _():
        def step(j, _):
            keys = pl.ds(pl.multiple_of(j * wide_keys, wide_keys), wide_keys)
            accumulate(keys, jnp.exp2(dot(qc[...], kvs[keys, :], 1, 1)), None)
            return 0

        lax.fori_loop(0, length // wide_keys, step, 0)

    @pl.when(jnp.logical_not(fast))
    def _():
        first = (meta[0] ^ (i * (ctx // heads))) * rows
        tok = first + lax.broadcasted_iota(jnp.int32, (rows, 1), 0)
        low, high = row_range(tok, meta, length)
        j_low = lax.div(row_range(first, meta, length)[0], fine_keys)
        j_high = lax.div(row_range(first + rows - 1, meta, length)[1] + fine_keys - 1, fine_keys)
        m = jnp.concatenate([shift[:, 0:1], shift[:, 64:65]], axis=0)

        def step(j, _):
            keys = pl.ds(pl.multiple_of(j * fine_keys, fine_keys), fine_keys)
            spot = j * fine_keys + lax.broadcasted_iota(jnp.int32, (1, fine_keys), 1)
            allowed = jnp.logical_and(spot >= low, spot < high)
            s = dot(qc[...], kvs[keys, :], 1, 1)
            e = jnp.where(allowed, jnp.exp2(s - m), 0.0)
            accumulate(keys, e, allowed)
            return 0

        lax.fori_loop(j_low, j_high, step, 0)

    a = dq_acc[...] * 0.125
    out = jnp.where(left, a[:half], pltpu.roll(a[half:], 64, 1)).astype(bf16)
    for c in range(heads):

        @pl.when(i == c)
        def _(c=c):
            dq_refs[c][...] = out

    @pl.when(i == heads - 1)
    def _():
        is_key = lax.broadcasted_iota(jnp.int32, (128, 1), 0) < 64
        for j in range(length // wide_keys):
            part = dkv_t[:, j * wide_keys : (j + 1) * wide_keys]
            part = jnp.where(is_key, part * math.log(2.0), part)
            dkv_n[j * wide_keys : (j + 1) * wide_keys, :] = part.T.astype(bf16)
        copies = []
        for k in range(ctx):
            at = pl.multiple_of((meta[0] ^ k) * rows, rows)
            target = dkv_refs[k % parts].at[pl.ds(k // parts * rows, rows)]
            copies.append(pltpu.make_async_copy(dkv_n.at[pl.ds(at, rows)], target, sems.at[k]))
        for c in copies:
            c.start()
        for c in copies:
            c.wait()


def proj_kernel(heads, tp, meta, *refs):
    o_refs, refs = refs[:heads], refs[heads:]
    weight, o_nat, *refs = refs
    pieces, (o_scr, x_scr) = refs[:tp], refs[tp:]
    half = o_refs[0].shape[0]
    for kh in range(heads):
        o_scr[meta[1] ^ kh] = o_refs[kh][...]
    for t in range(heads // 2):
        u, v = o_scr[2 * t].astype(f32), o_scr[2 * t + 1].astype(f32)
        o_nat[:half, t * 128 : (t + 1) * 128] = pair(u, v).astype(bf16)
        o_nat[half:, t * 128 : (t + 1) * 128] = pair_right(u, v).astype(bf16)
    x_scr[...] = dot(o_nat[...], weight[...], 1, 0)
    disperse(meta, x_scr, pieces)


def d_attn_kernel(heads, tp, meta, *refs):
    pieces, refs = refs[:tp], refs[tp:]
    weight, full, zero, *refs = refs
    zero[...] = jnp.zeros_like(zero)
    outs, (x_scr, d_scr) = refs[:heads], refs[heads:]
    half = outs[0].shape[0]
    assemble(meta, pieces, x_scr)
    x = x_scr[...].astype(bf16)
    full[...] = x
    for t in range(heads // 2):
        d = dot(x, weight[t * 128 : (t + 1) * 128, :], 1, 1)
        d_scr[2 * t] = pair(d[:half], d[half:]).astype(bf16)
        d_scr[2 * t + 1] = pair_right(d[:half], d[half:]).astype(bf16)
    for kh in range(heads):
        outs[kh][...] = d_scr[meta[1] ^ kh]


def d_qkv_kernel(heads, tp, half, meta, *refs):
    got, refs = refs[:heads], refs[heads:]
    weight, cosine, sine, normed, d_all, gain, *refs = refs
    pieces, (scr, x_scr) = refs[:tp], refs[tp:]
    every = heads * 64
    for kh in range(heads):
        scr[meta[1] ^ kh] = got[kh][...]
    for t in range(heads // 2):
        u, v = scr[2 * t].astype(f32), scr[2 * t + 1].astype(f32)
        dk, dv = pair(u[: 2 * half], v[: 2 * half]), pair_right(u[: 2 * half], v[: 2 * half])
        u, v = u[2 * half :], v[2 * half :]
        dq = jnp.concatenate([pair(u, v), pair_right(u, v)], axis=0)
        dq = dq * cosine[...] + rot_back(dq * sine[...])
        dk = dk * cosine[...] + rot_back(dk * sine[...])
        for n, d in enumerate((dq, dk, dv)):
            d_all[:, n * every + t * 128 : n * every + (t + 1) * 128] = d.astype(bf16)
    x_scr[...] = dot(d_all[...], weight[...], 1, 1)
    gain[...] = jnp.sum(x_scr[...] * normed[...].astype(f32), axis=0, keepdims=True)
    disperse(meta, x_scr, pieces)


def deal_kernel(orders, meta, grad, other, *outs):
    part, wide = grad.shape[0] // len(orders[0]), outs[0].shape[1]
    split = grad.shape[1] - wide
    deep = len(orders[0]) // 2
    for c, order in enumerate(orders):
        for n, k in enumerate(order):
            at = pl.ds(pl.multiple_of((meta[0] ^ k) * part, part), part)
            out, place = outs[2 * c + n // deep], pl.ds(n % deep * part, part)
            if c == 0:
                out[place, :] = grad[at, :wide].astype(bf16)
            else:
                out[place, :split] = grad[at, wide:].astype(bf16)
                out[place, split:] = other[at, :].astype(bf16)


def undeal_kernel(orders, meta, *refs):
    ins, (grad, other) = refs[:4], refs[4:]
    part, wide = grad.shape[0] // len(orders[0]), ins[0].shape[1]
    split = grad.shape[1] - wide
    deep = len(orders[0]) // 2
    for c, order in enumerate(orders):
        for n, k in enumerate(order):
            at = pl.ds(pl.multiple_of((meta[0] ^ k) * part, part), part)
            block = ins[2 * c + n // deep][n % deep * part : (n % deep + 1) * part, :].astype(f32)
            if c == 0:
                grad[at, :wide] = block
            else:
                grad[at, wide:] = block[:, :split]
                other[at, :] = block[:, split:]


def rope_tables(positions, width):
    freqs = jnp.exp(-(2.0 * jnp.arange(width // 2, dtype=f32) / width) * theta_log)
    angles = positions.astype(f32)[:, None] * freqs[None, :]
    cosine, sine = jnp.cos(angles), jnp.sin(angles)
    lay = lambda u: jnp.concatenate([u, u, u, u], axis=1)
    return lay(cosine), lay(sine)


def layer_norm(rows, gain):
    mean = jnp.mean(rows, axis=-1, keepdims=True)
    cent = rows - mean
    var = jnp.mean(cent * cent, axis=-1, keepdims=True)
    return cent * lax.rsqrt(var + 1e-05) * gain


def shards(
    hidden_in,
    norm1_gain,
    qkv_weight,
    attn_weight,
    norm2_gain,
    ffn_in_weight,
    ffn_out_weight,
    doc_ids,
    out_grad,
):
    seqs = hidden_in.shape[0]
    width = hidden_in.shape[2]
    heads = qkv_weight.shape[2]
    head_dim = qkv_weight.shape[3]
    rows = doc_ids.shape[1]
    half = rows // 2
    ff = ffn_out_weight.shape[0]
    ctx, tp = lax.axis_size("ctx"), lax.axis_size("tp")
    parts = ctx // heads
    length = ctx * rows
    own = rows // tp
    me, spot = lax.axis_index("ctx"), lax.axis_index("tp")
    sds = jax.ShapeDtypeStruct

    steps = jnp.arange(1, cut_count + 1, dtype=jnp.int32)
    counts = jnp.sum((doc_ids[:, :, None] < steps).astype(f32), axis=1)
    cuts = total(counts, "ctx").astype(jnp.int32)
    place = jnp.stack([me, me // parts, spot]).astype(jnp.int32)
    metas = [jnp.concatenate([place, cuts[s]]) for s in range(seqs)]

    every = heads * head_dim
    w_all = qkv_weight.reshape(width, 3 * every)
    w_out = attn_weight.reshape(every, width)
    w_in = ffn_in_weight.reshape(width, 2 * ff)
    tables = rope_tables(me * rows + jnp.arange(rows, dtype=jnp.int32), head_dim)
    scale = log2_e / math.sqrt(head_dim)

    resid = [hidden_in[s].astype(f32) for s in range(seqs)]
    full1, sents, mines = [], [], []

    def spread(s, zero):
        mine = mines[s]
        rest = jnp.concatenate([m[:rows] for m in mine], axis=0) + zero
        held = [(rest, [h * parts for h in range(heads)])]
        plan = [(h, 0, h * parts) for h in range(heads)]
        arrays = list(mine)
        for b in bit_list(parts):
            for block, ks in list(held):
                ks = [k ^ b for k in ks]
                held.append((swap(block, "ctx", b), ks))
                plan += [(len(arrays), n * rows, k) for n, k in enumerate(ks)]
                arrays.append(held[-1][0])
        return arrays, rest, plan

    for s in range(seqs):
        blocks = gather_blocks(layer_norm(resid[s], norm1_gain).astype(bf16))
        outs = call(
            functools.partial(qkv_kernel, heads, tp, half, scale),
            [place, *blocks, w_all, *tables],
            [sds((rows, width), bf16), sds((16, 128), bf16)]
            + [sds((rows + half, 128), bf16)] * heads,
            [
                pltpu.VMEM((rows, width), f32),
                pltpu.VMEM((heads, rows, 128), bf16),
                pltpu.VMEM((heads, half, 128), bf16),
            ],
            7,
            deps=[got[0][1]] if s else [cuts],
        )
        full1.append(outs[0])
        sent = outs[2:]
        sents.append(sent)
        sent_zero = outs[1][0, 0]
        mines.append([sent[0]] + [swap(sent[h], "ctx", h * parts) for h in range(1, heads)])
        if s == 0:
            got = [spread(0, jnp.zeros((), bf16))]

    smem = pl.BlockSpec(memory_space=pltpu.SMEM)
    hbm = pl.BlockSpec(memory_space=pl.ANY)
    small = pl.BlockSpec((half, 128), lambda i: (0, 0))
    tile = pl.BlockSpec((half, 128), lambda i: (i, 0))
    key_scratch = [
        pltpu.VMEM((length, 128), bf16),
        pltpu.VMEM((length, 128), bf16),
        pltpu.VMEM((heads, half, 128), bf16),
    ]
    sems = pltpu.SemaphoreType.DMA((ctx + heads,))

    def attend(s, chosen, deps):
        first = kept[s] is None
        ins = got[s][0] if first else [*mines[s], kept[s]]
        tiles = len(chosen)
        outs = call(
            functools.partial(
                attn_fwd_kernel, heads, ctx, rows, length, len(ins), plan if first else None, chosen
            ),
            [metas[s], *ins],
            [sds((half, 128), bf16)] * tiles
            + [sds((tiles * half, 128), f32)] * 2
            + [sds((8, 128), f32), sds((length if first else 16, 128), bf16)],
            key_scratch
            + [
                pltpu.VMEM((rows, 128), bf16),
                pltpu.VMEM((rows, 128), f32),
                pltpu.VMEM((rows, 128), f32),
                pltpu.SMEM((1,), f32),
                sems,
            ],
            2 + 9 * tiles * length / 6656,
            grid=(tiles,),
            in_specs=[smem] + [hbm] * len(ins),
            out_specs=[small] * tiles
            + [tile, tile, pl.BlockSpec((8, 128), lambda i: (0, 0)), hbm],
            deps=deps,
        )
        if first:
            kept[s] = outs[tiles + 3]
        for n, h in enumerate(chosen):
            o_mine[s][h] = outs[n]
            back[s][h] = outs[n] if h == 0 else swap(outs[n], "ctx", h * parts)
        scales[s].append((chosen, outs[tiles], outs[tiles + 1]))
        return outs[tiles + 2]

    def project(s, deps, notes):
        outs = call(
            functools.partial(proj_kernel, heads, tp),
            [place, *[back[s][h] for h in range(heads)], w_out],
            [sds((rows, every), bf16)] + [sds((own, width), bf16)] * tp,
            [pltpu.VMEM((heads, half, 128), bf16), pltpu.VMEM((rows, width), f32)],
            3,
            deps=deps,
        )
        o_nat[s] = outs[0]
        mid[s] = resid[s] + scatter_blocks(enumerate(outs[1:]), "tp", notes)

    def second_norm(s, zero):
        normed, pull_norm2[s] = jax.vjp(layer_norm, mid[s] + zero, norm2_gain)
        normed = normed.astype(bf16)
        blocks = gather_blocks(normed)
        full2[s] = jnp.concatenate(blocks, axis=0)
        return normed, blocks[2]

    many = range(seqs)
    kept, o_nat, mid = [None] * seqs, [None] * seqs, [None] * seqs
    full2, pull_norm2 = [None] * seqs, [None] * seqs
    o_mine, back, scales = [{} for _ in many], [{} for _ in many], [[] for _ in many]
    plan = got[0][2]
    grads_all = (out_grad + sent_zero).reshape(seqs * own, width)
    grad_blocks = gather_blocks(grads_all)
    grads_all = jnp.concatenate(grad_blocks, axis=0).reshape(tp, seqs, own, width)
    grads_all = grads_all.transpose(1, 0, 2, 3).reshape(seqs * rows, width)
    got.append(spread(1, jnp.zeros((), bf16)))
    mark = attend(0, list(range(heads)), [got[1][1], grad_blocks[2]])
    mark = attend(1, list(range(heads - 1, heads)), [mark])
    notes = []
    project(0, [mark], notes)
    waits = [notes[0][0]]
    for n, h in enumerate(reversed(range(heads - 1))):
        mark = attend(1, [h], [mark, *waits])
        if n == 0:
            waits = second_norm(0, mark[0, 0])
            waits, later = [waits[0]], [waits[1]]
        else:
            waits, later = later, []
    notes = []
    project(1, [mark], notes)
    full2[0] = full2[0] + gate(notes[0][0])
    last_rows = second_norm(1, 0.0)[1]

    acts, d_mid, d_pieces, gain2 = [], [], [], 0.0

    def to_heads(s, deps):
        outs = call(
            functools.partial(d_attn_kernel, heads, tp),
            [place, *d_pieces[s], w_out],
            [sds((rows, width), bf16), sds((16, 128), bf16)] + [sds((half, 128), bf16)] * heads,
            [pltpu.VMEM((rows, width), f32), pltpu.VMEM((heads, half, 128), bf16)],
            4,
            deps=deps,
        )
        d = outs[2:]
        d = [d[0]] + [swap(d[h], "ctx", h * parts) for h in range(1, heads)]
        return outs[0], d, outs[1][0, 0]

    zero = gate(last_rows)
    g_out_w, g_in_w = 0.0, 0.0
    for s in range(seqs):
        upper = dot(full2[s], w_in, 1, 0)
        grads = grads_all[s * rows : (s + 1) * rows]
        gated, pull_gelu = jax.vjp(
            lambda a, b: jax.nn.gelu(a, approximate=False) * b, upper[:, :ff], upper[:, ff:]
        )
        act = gated.astype(bf16)
        d_act = dot(grads, ffn_out_weight, 1, 1)
        d_upper = jnp.concatenate(pull_gelu(d_act), axis=1).astype(bf16)
        d_part = dot(d_upper + zero, w_in, 1, 1).astype(bf16)
        notes = []
        d_normed2 = scatter_blocks(
            {j: d_part[j * own : (j + 1) * own] for j in range(tp)}, "tp", notes
        )
        g_out_w = g_out_w + dot(act, grads, 0, 0)
        g_in_w = g_in_w + dot(d_upper, full2[s], 0, 0)
        if s == seqs - 1:
            g_in_w = g_in_w.astype(bf16)
            d_normed2 = d_normed2 + gate(g_in_w).astype(f32)
        d_mid_norm, d_gain = pull_norm2[s](d_normed2)
        gain2 = gain2 + d_gain
        d_mid.append(out_grad[s].astype(f32) + d_mid_norm)
        d_pieces.append(gather_blocks(d_mid[s].astype(bf16)))
        if s == 0:
            dmid_full, d_attn, zero = to_heads(0, [g_in_w, g_out_w])
            g_attn_w = dot(dmid_full, o_nat[0], 0, 0)
        acts.append(act)
    later_dmid, later_attn, _ = to_heads(1, [])
    d_attns = [d_attn, later_attn]
    g_attn_w = g_attn_w + dot(later_dmid, o_nat[1], 0, 0)
    g_out_w = g_out_w + gate(d_attn[heads - 1]).astype(f32)
    ready = [g.astype(bf16) for g in (g_in_w, g_out_w)]
    early = lax.psum(ready, "ctx")
    ready = [g[:16, :128] for g in ready] + [later_dmid]

    in_grad, gain1, zeros, d_got = [], 0.0, [], []
    backward_cost = [1, 1]
    for s in range(seqs):
        outs = call(
            functools.partial(
                attn_bwd_kernel, heads, ctx, rows, length, [g[0] for g in scales[s]]
            ),
            [
                metas[s],
                *d_attns[s],
                *[o_mine[s][h] for h in range(heads)],
                *[g[1] for g in scales[s]],
                *[g[2] for g in scales[s]],
                *mines[s],
                kept[s],
            ],
            [sds((half, 128), bf16)] * heads
            + [sds((heads * rows, 128), bf16)] * parts
            + [sds((16, 128), bf16)],
            key_scratch
            + [
                pltpu.VMEM((heads, half, 128), bf16),
                pltpu.VMEM((heads, half, 128), bf16),
                pltpu.VMEM((heads * half, 128), f32),
                pltpu.VMEM((heads * half, 128), f32),
                pltpu.VMEM((rows, 128), bf16),
                pltpu.VMEM((rows, 128), bf16),
                pltpu.VMEM((64, rows), bf16),
                pltpu.VMEM((64, rows), bf16),
                pltpu.VMEM((rows, 128), f32),
                pltpu.VMEM((128, length), f32),
                pltpu.VMEM((length, 128), bf16),
                sems,
            ],
            backward_cost[s],
            grid=(heads,),
            in_specs=[smem]
            + [small] * (2 * heads)
            + [pl.BlockSpec((len(g[0]) * half, 128), lambda i: (0, 0)) for g in scales[s]] * 2
            + [hbm] * (heads + 1),
            out_specs=[small] * heads
            + [hbm] * parts
            + [pl.BlockSpec((16, 128), lambda i: (0, 0))],
            deps=ready,
        )
        ready = [outs[0]]
        if s == seqs - 1:
            act = jnp.concatenate(acts, axis=0) + outs[-1][0, 0]
        zeros.append(outs[-1][0, 0])
        d_got.append((outs[:heads], scatter_blocks(enumerate(outs[heads:-1]), "ctx")))
    sent = []
    for dq, dkv in d_got:
        dkv = dkv + zeros[-1].astype(f32)
        sent.append(
            [
                jnp.concatenate([dkv[h * rows : (h + 1) * rows].astype(bf16), dq[h]], axis=0)
                for h in range(heads)
            ]
        )
    backs = [
        [sent[s][0]] + [swap(sent[s][h], "ctx", h * parts) for h in range(1, heads)] for s in many
    ]
    out_part = dot(act, ffn_out_weight, 1, 0).astype(bf16).reshape(seqs, tp, own, width)
    ffn_sum = scatter_blocks({j: out_part[:, j] for j in range(tp)})
    block_out = (jnp.stack(mid) + ffn_sum).astype(bf16)

    g_qkv_w = 0.0
    for s in range(seqs):
        back = backs[s]
        outs = call(
            functools.partial(d_qkv_kernel, heads, tp, half),
            [place, *back, w_all, *tables, full1[s]],
            [sds((rows, 3 * every), bf16), sds((1, width), f32)]
            + [sds((own, width), bf16)] * tp,
            [pltpu.VMEM((heads, rows + half, 128), bf16), pltpu.VMEM((rows, width), f32)],
            6,
            deps=[*early, g_qkv_w, in_grad[0]] if s else [backs[1][1], block_out],
        )
        g_qkv_w = g_qkv_w + dot(full1[s], outs[0], 0, 0)
        gain1 = gain1 + outs[1][0]
        _, pull_norm1 = jax.vjp(lambda r: layer_norm(r, norm1_gain), resid[s])
        d_in_norm = pull_norm1(scatter_blocks(enumerate(outs[2:])))[0]
        in_grad.append((d_mid[s] + d_in_norm).astype(bf16))
    orders = [row_order(ctx, turn) for turn in range(2)]
    dealt = call(
        functools.partial(deal_kernel, [o[1] for o in orders]),
        [place, g_qkv_w, g_attn_w],
        [sds((width // 2, 2 * every), bf16)] * 4,
        [],
        3,
    )
    sums = []
    for turn in range(2):
        ends, reduced = sum_halves(dealt[2 * turn], dealt[2 * turn + 1], "ctx", orders[turn][0])
        sums += ends
    g_qkv_w, g_attn_w = call(
        functools.partial(undeal_kernel, [o[1] for o in orders]),
        [place, *sums],
        [sds((width, 3 * every), f32), sds((width, every), f32)],
        [],
        3,
    )
    g_qkv_w = g_qkv_w.reshape(width, 3, heads, head_dim)

    gains = jnp.stack([gain1 / norm1_gain, gain2]) + gate(reduced).astype(f32)
    gains = total(total(gains, "tp"), "ctx")
    return (
        block_out,
        jnp.stack(in_grad),
        gains[0],
        g_qkv_w,
        g_attn_w.T.reshape(heads, head_dim, width),
        gains[1],
        early[0].astype(f32).T.reshape(width, 2, ff),
        early[1].astype(f32),
    )


def solution(mesh):
    in_specs = (
        P(None, ("ctx", "tp"), None),
        P(),
        P(None, None, "tp", None),
        P("tp", None, None),
        P(),
        P(None, None, "tp"),
        P("tp", None),
        P(None, "ctx"),
        P(None, ("ctx", "tp"), None),
    )
    out_specs = (
        P(None, ("ctx", "tp"), None),
        P(None, ("ctx", "tp"), None),
        P(),
        P(None, None, "tp", None),
        P("tp", None, None),
        P(),
        P(None, None, "tp"),
        P("tp", None),
    )
    return jax.shard_map(shards, mesh=mesh, in_specs=in_specs, out_specs=out_specs, check_vma=False)
```
